256 devices in a mesh: space: 32 (over y, z), tm: 8 (over x, core).
Axes of the slice: x: 4, y: 4, z: 8, core: 2. Of those that a mesh axis runs over, the one named last changes fastest.
Arguments:
- fine_residual: bfloat16 [16, 64, 4, 8, 32, 128], P('tm', 'space'), may hold values from -12 to 12
- restriction: bfloat16 [16, 64, 4, 8, 128, 128], P('tm', 'space'), may hold values from -0.25 to 0.25
- coarse_links: bfloat16 [8, 32, 2, 4, 9, 128, 128], P('tm', 'space'), may hold values from -1 to 12.5
- plane_owner: int32 [32], replicated, may hold values from 0 to 31, as said below
Outputs:
- correction: float32 [16, 64, 4, 8, 32, 128], P('tm', 'space')
- coarse_residual: float32 [8, 32, 2, 4, 32, 128], P('tm', 'space')
The draws below stay inside these ranges and needn't reach their ends.
Inputs may be any that keep to these rules, and one draw needn't show every extreme that they name: `plane_owner`: every coarse plane is named by exactly one owner, and for some plane z the owner at index (z + 16) mod 32 names z.
All inputs are finite; a program needn't handle non-finite values.
Results may differ from the reference program's by a relative error of at most 0.009.
Values may be sent and summed in bfloat16 or wider, within the bound.
A program may use at most 64 MiB of HBM per device.

```python
import math
import jax
import jax.numpy as jnp
from jax import lax

W = 128
LY = 2
LX = 4
NRHS = 32
ITERS = 3
NT_C = 8
NZ_C = 32
NT_F = 16
NZ_F = 64
FY = 4
FX = 8


def draw_fine_residual(key, part):
    key = jax.random.fold_in(key, 11)
    shape = (NT_F, NZ_F, FY, FX, NRHS, W)
    depth = jnp.arange(NZ_F, dtype=jnp.float32) / max(NZ_F - 1, 1)
    rising = jnp.exp(math.log(3.0) * depth)[None, :, None, None, None, None]
    value = jnp.clip(jax.random.normal(key, shape, jnp.float32), -4.0, 4.0) * rising
    return value.astype(jnp.bfloat16)


def draw_coarse_links(key, part):
    key = jax.random.fold_in(key, 23)
    shape = (NT_C, NZ_C, LY, LX, 9, W, W)
    first_key, second_key = jax.random.split(key, 2)
    spread = 0.3 / math.sqrt(W)
    hopping = jnp.clip(jax.random.normal(first_key, shape, jnp.float32), -4.0, 4.0) * spread
    zpos = jnp.arange(NZ_C, dtype=jnp.float32) / max(NZ_C - 1, 1)
    tpos = jnp.arange(NT_C, dtype=jnp.float32) / max(NT_C - 1, 1)
    level = jnp.exp(math.log(2.0) * tpos)[:, None] * jnp.exp(math.log(3.0) * zpos)[None, :]
    level = level.reshape(NT_C, NZ_C, 1, 1, 1, 1, 1)
    channel = jnp.exp(jax.random.uniform(second_key, (NT_C, NZ_C, LY, LX, 1, W, 1), jnp.float32, math.log(1.6), math.log(2.0)))
    diagonal = level * channel
    selfmask = (jnp.arange(9)[:, None, None] == 0) & (jnp.arange(W)[None, :, None] == jnp.arange(W)[None, None, :])
    value = hopping + diagonal * selfmask.astype(jnp.float32)
    return value.astype(jnp.bfloat16)


def draw_plane_owner(key, part):
    key = jax.random.fold_in(key, 37)
    first_key, second_key = jax.random.split(key, 2)
    seats = jnp.arange(NZ_C, dtype=jnp.int32)
    shuffled = jax.random.permutation(first_key, seats).astype(jnp.int32)
    chosen = jax.random.randint(second_key, (), 0, NZ_C).astype(jnp.int32)
    target = ((chosen + NZ_C // 2) % NZ_C).astype(jnp.int32)
    holder = jnp.sum(jnp.where(shuffled == chosen, seats, 0)).astype(jnp.int32)
    displaced = jnp.sum(jnp.where(seats == target, shuffled, 0)).astype(jnp.int32)
    value = jnp.where(seats == target, chosen, jnp.where(seats == holder, displaced, shuffled))
    return value.astype(jnp.int32)


def block_levels(key, shape, pieces, smallest, top_value):
    def one(dim, shards_of):
        draws = jax.random.uniform(jax.random.fold_in(jax.random.fold_in(key, 6), dim), (shards_of,), jnp.float32, smallest / len(pieces), top_value / len(pieces))
        return jnp.repeat(jnp.exp(draws), shape[dim] // shards_of).reshape((-1,) + (1,) * (len(shape) - dim - 1))

    factor_of = one(*pieces[0])
    for cut in pieces[1:]:
        factor_of = factor_of * one(*cut)
    return factor_of


def noise(own_key, extent, deviation, most, cuts=(), held_as=jnp.bfloat16):
    array = jax.random.normal(own_key, extent, jnp.float32) * deviation
    if len(cuts) > 0:
        array = block_levels(own_key, extent, cuts, -0.22, 0.18) * array
    return jnp.clip(array, min=-most, max=most).astype(held_as)


def setup_inputs(seed: int = 0) -> dict:
    key_list = jax.random.split(jax.random.key(seed), 5)
    return {
        "fine_residual": draw_fine_residual(jax.random.fold_in(key_list[4], 71), 0),
        "restriction": noise(key_list[1], (NT_F, NZ_F, FY, FX, W, W), (4 * W) ** -0.5, 0.25, ((0, 8), (1, 32))),
        "coarse_links": draw_coarse_links(jax.random.fold_in(key_list[4], 71), 0),
        "plane_owner": draw_plane_owner(jax.random.fold_in(key_list[4], 71), 0),
    }


def inner_sum(left, right):
    return jnp.sum(left * right, axis=(0, 1, 2, 3, 5))


def coarse_apply(vector, coarse_links):
    neighbours = [vector, jnp.roll(vector, -1, 0), jnp.roll(vector, 1, 0), jnp.roll(vector, -1, 1), jnp.roll(vector, 1, 1), jnp.roll(vector, -1, 2), jnp.roll(vector, 1, 2), jnp.roll(vector, -1, 3), jnp.roll(vector, 1, 3)]
    total = jnp.zeros(vector.shape, jnp.float32)
    for direction in range(9):
        total = total + jnp.einsum("tzyxnj,tzyxji->tzyxni", neighbours[direction].astype(jnp.float32), coarse_links[:, :, :, :, direction].astype(jnp.float32), precision=lax.Precision.HIGHEST)
    return total


def restrict_slice(pair):
    fine_rows, maps = pair
    products = jnp.einsum("abcdnj,abcdji->abcdni", fine_rows.astype(jnp.float32), maps.astype(jnp.float32), precision=lax.Precision.HIGHEST)
    blocks = products.reshape(2, NZ_C, 2, LY, 2, LX, 2, NRHS, W)
    return jnp.sum(blocks, axis=(0, 2, 4, 6))


def prolong_slice(pair):
    fix_plane, maps = pair
    expanded = jnp.broadcast_to(fix_plane[None, :, None, :, None, :, None], (2, NZ_C, 2, LY, 2, LX, 2, NRHS, W)).reshape(2, NZ_F, FY, FX, NRHS, W)
    return jnp.einsum("abcdni,abcdji->abcdnj", expanded.astype(jnp.float32), maps.astype(jnp.float32), precision=lax.Precision.HIGHEST)


def reference(fine_residual, restriction, coarse_links, plane_owner):
    fine_split = fine_residual.reshape(NT_C, 2, NZ_F, FY, FX, NRHS, W)
    maps_split = restriction.reshape(NT_C, 2, NZ_F, FY, FX, W, W)
    owner_rhs = lax.map(restrict_slice, (fine_split, maps_split))
    seats = jnp.arange(NZ_C, dtype=jnp.int32)
    source = jnp.sum(jnp.where(plane_owner[:, None] == seats[None, :], seats[:, None], 0), axis=0).astype(jnp.int32)
    residual = jnp.take(owner_rhs, source, axis=1)
    solution = jnp.zeros_like(residual)
    basis_dirs = []
    basis_imgs = []
    basis_norms = []
    for iteration in range(ITERS):
        direction = residual.astype(jnp.bfloat16)
        images = coarse_apply(direction, coarse_links)
        factors = [inner_sum(basis_imgs[earlier], images) / basis_norms[earlier] for earlier in range(iteration)]
        search = direction.astype(jnp.float32)
        search_img = images
        for earlier in range(iteration):
            search = search - factors[earlier][:, None] * basis_dirs[earlier]
            search_img = search_img - factors[earlier][:, None] * basis_imgs[earlier]
        norm_now = inner_sum(search_img, search_img)
        step_size = inner_sum(search_img, residual) / norm_now
        solution = solution + step_size[:, None] * search
        residual = residual - step_size[:, None] * search_img
        basis_dirs.append(search)
        basis_imgs.append(search_img)
        basis_norms.append(norm_now)
    fix_field = solution.astype(jnp.bfloat16)
    owner_fix = jnp.take(fix_field, plane_owner, axis=1)
    correction = lax.map(prolong_slice, (owner_fix, maps_split)).reshape(NT_F, NZ_F, FY, FX, NRHS, W)
    return correction, residual
```

```python
import jax
import jax.numpy as jnp
from jax import lax
from jax.experimental import pallas as pl
from jax.experimental.pallas import tpu as pltpu
from jax.sharding import PartitionSpec as P

ITERS = 3
NS = 32
NT = 8
NZ = 8
CS = 8
RHS = 32
W = 128
F32 = jnp.float32
BF16 = jnp.bfloat16
MESH = pl.DeviceIdType.MESH


def dot(a, b):
    return jnp.dot(a, b, preferred_element_type=F32)


def kernel(
    owner_ref, fine_ref, restr_ref, links_ref, corr_ref, res_ref,
    fine_v, restr_v, links_v, out_v,
    own_v, mid_v, pick_v, r_v, p_v, halo_v, img_v,
    midb_v, pickb_v, back_v, part_v, sumt_v, sums_v, source_s,
    fine_sem, restr_sem, links_sem, out_sem,
    up_send, up_recv, down_send, down_recv,
    halo_send, halo_recv, t_send, t_recv, s_send, s_recv,
    b1_send, b1_recv, b2_send, b2_recv,
):
    me = lax.axis_index("space")
    tm = lax.axis_index("tm")
    my_y, my_z = me // NZ, me % NZ

    def site_of(step):
        return lax.rem(my_z + 1 + step, CS)

    def fine_copies(step):
        cs = site_of(step)
        y, x = cs // 4, cs % 4
        sl = (slice(None), slice(None), pl.ds(2 * y, 2), pl.ds(2 * x, 2))
        return (
            pltpu.make_async_copy(fine_ref.at[sl], fine_v.at[cs], fine_sem.at[step]),
            pltpu.make_async_copy(restr_ref.at[sl], restr_v.at[cs], restr_sem.at[step]),
        )

    for step in range(CS):
        for c in fine_copies(step):
            c.start()
    links_copy = pltpu.make_async_copy(links_ref.at[0, 0], links_v, links_sem)
    links_copy.start()

    barrier = pltpu.get_barrier_semaphore()
    for d in range(1, NS):
        pl.semaphore_signal(
            barrier, inc=1, device_id={"space": lax.rem(me + d, NS)}, device_id_type=MESH)
    for d in range(1, NT):
        pl.semaphore_signal(
            barrier, inc=1, device_id={"tm": lax.rem(tm + d, NT)}, device_id_type=MESH)

    def find(z, carry):
        acc = jnp.int32(0)
        for s in range(NS):
            acc = jnp.where(owner_ref[s] == z, s, acc)
        source_s[z] = acc
        return carry

    lax.fori_loop(0, NS, find, 0)
    pl.semaphore_wait(barrier, NS - 1 + NT - 1)

    for step in range(CS):
        for c in fine_copies(step):
            c.wait()
        cs = site_of(step)
        acc = jnp.zeros((RHS, W), F32)
        for a in range(2):
            for b in range(2):
                for c in range(2):
                    lhs = jnp.concatenate(
                        [fine_v[cs, a, b, c, 0], fine_v[cs, a, b, c, 1]], axis=-1)
                    acc = acc + dot(lhs, restr_v[cs, a, b, c].reshape(2 * W, W))
        own_v[pl.ds(cs * 4, 4)] = acc.reshape(4, 8, W)
        for q in range(4):
            target = q * NZ + cs

            def send(q=q, target=target, cs=cs):
                pltpu.make_async_remote_copy(
                    src_ref=own_v.at[cs * 4 + q], dst_ref=mid_v.at[me],
                    send_sem=up_send, recv_sem=up_recv,
                    device_id={"space": target}, device_id_type=MESH).start()

            if step < CS - 1:
                send()
            else:
                pl.when(q != my_y)(send)
    my_slot = my_z * 4 + my_y
    mid_v[me] = own_v[my_slot]

    def drain(ref, sem):
        pltpu.make_async_copy(ref, ref, sem).wait()

    others = pl.ds(0, NS - 1)
    drain(mid_v.at[others], up_recv)

    for d in range(1, NS):
        target = lax.rem(me + d, NS)
        pick_v[d] = mid_v[source_s[target]]
        pltpu.make_async_remote_copy(
            src_ref=pick_v.at[d], dst_ref=r_v.at[my_slot],
            send_sem=down_send, recv_sem=down_recv,
            device_id={"space": target}, device_id_type=MESH).start()
    r_v[my_slot] = mid_v[source_s[me]]
    drain(r_v.at[others], down_recv)
    links_copy.wait()

    lane = lax.broadcasted_iota(jnp.int32, (RHS, W), 1)
    row = lax.broadcasted_iota(jnp.int32, (RHS, W), 0)

    def read_r(cs):
        return r_v[pl.ds(4 * cs, 4)].reshape(RHS, W)

    def back_up(it):
        for h in range(16):
            target = 2 * h + it - 1

            @pl.when(target != me)
            def _():
                pltpu.make_async_remote_copy(
                    src_ref=p_v.at[it, h // 2, pl.ds(16 * (h % 2), 16)],
                    dst_ref=midb_v.at[me],
                    send_sem=b1_send.at[it - 1], recv_sem=b1_recv,
                    device_id={"space": target}, device_id_type=MESH).start()

            @pl.when(target == me)
            def _():
                midb_v[me] = p_v[it, h // 2, pl.ds(16 * (h % 2), 16)]

    def back_down(it):
        @pl.when(me % 2 == it - 1)
        def _():
            drain(midb_v.at[others], b1_recv)
            piece = me // 2
            for d in range(1, NS):
                target = lax.rem(me + d, NS)
                pickb_v[d] = midb_v[owner_ref[target]]
                pltpu.make_async_remote_copy(
                    src_ref=pickb_v.at[d], dst_ref=back_v.at[it - 1, piece],
                    send_sem=b2_send, recv_sem=b2_recv.at[it - 1],
                    device_id={"space": target}, device_id_type=MESH).start()
            back_v[it - 1, piece] = midb_v[owner_ref[me]]

    halo_to = (
        {"tm": lax.rem(tm + NT - 1, NT)}, {"tm": lax.rem(tm + 1, NT)},
        {"space": lax.rem(me + NS - 1, NS)}, {"space": lax.rem(me + 1, NS)},
    )

    def halo_copy(it, k):
        return pltpu.make_async_remote_copy(
            src_ref=p_v.at[it], dst_ref=halo_v.at[it, k],
            send_sem=halo_send.at[it, k], recv_sem=halo_recv.at[it, k],
            device_id=halo_to[k], device_id_type=MESH)

    norms, alphas, betas = [], [], []
    for it in range(ITERS):
        for cs in range(CS):
            p_v[it, cs] = read_r(cs).astype(BF16)
        for k in range(4):
            halo_copy(it, k).start()
        if it > 0:
            back_up(it)
        for cs in range(CS):
            y, x = cs // 4, cs % 4
            vy = p_v[it, (1 - y) * 4 + x]
            lhs = jnp.concatenate(
                [vy, vy, p_v[it, y * 4 + (x + 1) % 4], p_v[it, y * 4 + (x + 3) % 4]], axis=-1)
            img_v[it, cs] = dot(lhs, links_v[y, x, pl.ds(5, 4)].reshape(4 * W, W)) + dot(
                p_v[it, cs], links_v[y, x, 0])
        for k in range(4):
            halo_copy(it, k).wait_recv()
        nprod = it + 2
        prods = [jnp.zeros((RHS, W), F32) for _ in range(nprod)]
        for cs in range(CS):
            y, x = cs // 4, cs % 4
            lhs = jnp.concatenate([halo_v[it, k, cs] for k in range(4)], axis=-1)
            q = img_v[it, cs] + dot(lhs, links_v[y, x, pl.ds(1, 4)].reshape(4 * W, W))
            img_v[it, cs] = q
            factors = [img_v[j, cs] for j in range(it)] + [q, read_r(cs)]
            for k in range(nprod):
                prods[k] = prods[k] + q * factors[k]
        packed = jnp.zeros((RHS, W), F32)
        for k in range(nprod):
            total = jnp.sum(prods[k], axis=1, keepdims=True)
            packed = packed + jnp.where(lane == row + RHS * k, total, 0.0)
        mine = jnp.sum(packed, axis=0, keepdims=True)

        part_v[it, 0] = mine
        sumt_v[it, tm] = mine
        for d in range(1, NT):
            pltpu.make_async_remote_copy(
                src_ref=part_v.at[it, 0], dst_ref=sumt_v.at[it, tm],
                send_sem=t_send.at[it], recv_sem=t_recv.at[it],
                device_id={"tm": lax.rem(tm + d, NT)}, device_id_type=MESH).start()
        if it > 0:
            back_down(it)
        drain(sumt_v.at[it, pl.ds(0, NT - 1)], t_recv.at[it])
        over_t = jnp.sum(sumt_v[it], axis=0)
        part_v[it, 1] = over_t
        sums_v[it, me] = over_t
        for d in range(1, NS):
            pltpu.make_async_remote_copy(
                src_ref=part_v.at[it, 1], dst_ref=sums_v.at[it, me],
                send_sem=s_send.at[it], recv_sem=s_recv.at[it],
                device_id={"space": lax.rem(me + d, NS)}, device_id_type=MESH).start()
        drain(sums_v.at[it, others], s_recv.at[it])
        totals = jnp.broadcast_to(jnp.sum(sums_v[it], axis=0), (RHS, W))
        cols = [
            jnp.sum(jnp.where(lane == row + RHS * k, totals, 0.0), axis=1, keepdims=True)
            for k in range(nprod)
        ]
        beta = [cols[j] / norms[j] for j in range(it)]
        norm = cols[it]
        for j in range(it):
            norm = norm - beta[j] * cols[j]
        alpha = cols[it + 1] / norm
        norms.append(norm)
        alphas.append(alpha)
        betas.append(beta)
        for cs in range(CS):
            q = img_v[it, cs]
            for j in range(it):
                q = q - beta[j] * img_v[j, cs]
            img_v[it, cs] = q
            new = read_r(cs) - alpha * q
            if it < ITERS - 1:
                r_v[pl.ds(4 * cs, 4)] = new.reshape(4, 8, W)
            else:
                res_ref[0, 0, cs // 4, cs % 4] = new

    c2 = alphas[2]
    c1 = alphas[1] - alphas[2] * betas[2][1]
    c0 = alphas[0] - c1 * betas[1][0] - alphas[2] * betas[2][0]

    for it in (1, 2):
        @pl.when(me % 2 == it - 1)
        def _():
            drain(back_v.at[it - 1, pl.ds(0, 15)], b2_recv.at[it - 1])

        @pl.when(me % 2 != it - 1)
        def _():
            drain(back_v.at[it - 1], b2_recv.at[it - 1])

    out_copies = []
    for cs in range(CS):
        y, x = cs // 4, cs % 4
        own = own_v[pl.ds(4 * cs, 4)].reshape(RHS, W).astype(BF16).astype(F32)
        d1 = back_v[0, pl.ds(2 * cs, 2)].reshape(RHS, W).astype(F32)
        d2 = back_v[1, pl.ds(2 * cs, 2)].reshape(RHS, W).astype(F32)
        fix = (c0 * own + c1 * d1 + c2 * d2).astype(BF16)
        for a in range(2):
            for b in range(2):
                for c in range(2):
                    both = lax.dot_general(
                        fix, restr_v[cs, a, b, c].reshape(2 * W, W),
                        (((1,), (1,)), ((), ())), preferred_element_type=F32)
                    out_v[cs, a, b, c, 0] = both[:, :W]
                    out_v[cs, a, b, c, 1] = both[:, W:]
        copy = pltpu.make_async_copy(
            out_v.at[cs],
            corr_ref.at[:, :, pl.ds(2 * y, 2), pl.ds(2 * x, 2)], out_sem.at[cs])
        copy.start()
        out_copies.append(copy)

    drain(own_v.at[others], up_send)
    drain(pick_v.at[others], down_send)
    for it in range(ITERS):
        for k in range(4):
            halo_copy(it, k).wait_send()
        drain(sumt_v.at[it, pl.ds(0, NT - 1)], t_send.at[it])
        drain(sums_v.at[it, others], s_send.at[it])
    for it in (1, 2):
        @pl.when(me % 2 == it - 1)
        def _():
            drain(back_v.at[it - 1, pl.ds(0, 15)], b1_send.at[it - 1])

        @pl.when(me % 2 != it - 1)
        def _():
            drain(back_v.at[it - 1], b1_send.at[it - 1])
    drain(pickb_v.at[others], b2_send)
    for copy in out_copies:
        copy.wait()


def body(fine_residual, restriction, coarse_links, plane_owner):
    dma = pltpu.SemaphoreType.DMA
    anyspec = pl.BlockSpec(memory_space=pl.ANY)
    return pl.pallas_call(
        kernel,
        out_shape=(
            jax.ShapeDtypeStruct(fine_residual.shape, F32),
            jax.ShapeDtypeStruct((1, 1, 2, 4, RHS, W), F32),
        ),
        in_specs=[pl.BlockSpec(memory_space=pltpu.SMEM), anyspec, anyspec, anyspec],
        out_specs=(anyspec, pl.BlockSpec(memory_space=pltpu.VMEM)),
        scratch_shapes=[
            pltpu.VMEM((CS, 2, 2, 2, 2, RHS, W), BF16),
            pltpu.VMEM((CS, 2, 2, 2, 2, W, W), BF16),
            pltpu.VMEM((2, 4, 9, W, W), BF16),
            pltpu.VMEM((CS, 2, 2, 2, 2, RHS, W), F32),
            pltpu.VMEM((NS, 8, W), F32),
            pltpu.VMEM((NS, 8, W), F32),
            pltpu.VMEM((NS, 8, W), F32),
            pltpu.VMEM((NS, 8, W), F32),
            pltpu.VMEM((ITERS, CS, RHS, W), BF16),
            pltpu.VMEM((ITERS, 4, CS, RHS, W), BF16),
            pltpu.VMEM((ITERS, CS, RHS, W), F32),
            pltpu.VMEM((NS, 16, W), BF16),
            pltpu.VMEM((NS, 16, W), BF16),
            pltpu.VMEM((2, 16, 16, W), BF16),
            pltpu.VMEM((ITERS, 2, 1, W), F32),
            pltpu.VMEM((ITERS, NT, 1, W), F32),
            pltpu.VMEM((ITERS, NS, 1, W), F32),
            pltpu.SMEM((NS,), jnp.int32),
            dma((CS,)), dma((CS,)), dma(()), dma((CS,)),
            dma(()), dma(()), dma(()), dma(()),
            dma((ITERS, 4)), dma((ITERS, 4)),
            dma((ITERS,)), dma((ITERS,)), dma((ITERS,)), dma((ITERS,)),
            dma((2,)), dma(()), dma(()), dma((2,)),
        ],
        compiler_params=pltpu.CompilerParams(
            collective_id=0, has_side_effects=True, vmem_limit_bytes=60 * 1024 * 1024),
        name="coarse_correction",
    )(plane_owner, fine_residual, restriction, coarse_links)


def solution(mesh):
    placed = (
        P("tm", "space", None, None, None, None),
        P("tm", "space", None, None, None, None),
        P("tm", "space", None, None, None, None, None),
        P(),
    )
    return jax.shard_map(
        body,
        mesh=mesh,
        in_specs=placed,
        out_specs=(
            P("tm", "space", None, None, None, None),
            P("tm", "space", None, None, None, None),
        ),
        check_vma=False,
    )
```

```python
import jax
import jax.numpy as jnp
from jax import lax
from jax.experimental import pallas as pl
from jax.experimental.pallas import tpu as pltpu
from jax.sharding import PartitionSpec as P

ITERS = 3
NS = 32
NT = 8
NY, NZ = 4, 8
CHIPS = NS * NT // 2
CS = 8
RHS = 32
W = 128
F32 = jnp.float32
BF16 = jnp.bfloat16
MESH = pl.DeviceIdType.MESH
MIB = 1024 * 1024


def dot(a, b):
    return jnp.dot(a, b, preferred_element_type=F32)


def drain(ref, sem):
    pltpu.make_async_copy(ref, ref, sem).wait()


def far_first(i, n):
    return n // 2 + (1 - 2 * (i % 2)) * ((i + 1) // 2)


def cycle_kernel(
    owner_hbm, fine_ref, restr_ref, links_ref, fix_ref, res_ref,
    fine_v, restr_v, links_v, fix_v, res_v,
    own_v, mid_v, pick_v, r_v, low_v, p_v, img_v, orth_v,
    ph_v, lowh_v, imgh_v, rh_v,
    midq0_v, midq1_v, pickq_v, backq_v, part_v, pair_v, sums_v, owner_ref, source_s,
    owner_sem, fix_sem, res_sem, fine_sem, restr_sem, links_sem,
    up_send, up_recv, down_send, down_recv,
    p_send, p_recv, low_send, low_recv, img_send, img_recv,
    c_send, c_recv, s_send, s_recv, b1_send, b1_recv, b2_send, b2_recv,
):
    me = lax.axis_index("space")
    tm = lax.axis_index("tm")
    my_y, my_z = me // NZ, me % NZ
    my_x, my_c = tm // 2, tm % 2

    def space_far(d):
        dz, dy = far_first(d // NY, NZ), far_first(d % NY, NY)
        return lax.rem(my_y + dy, NY) * NZ + lax.rem(my_z + dz, NZ)

    def site_of(step):
        return lax.rem(my_z + far_first(step, NZ), CS)

    def fine_copies(step):
        cs = site_of(step)
        y, x = cs // 4, cs % 4
        sl = (slice(None), slice(None), pl.ds(2 * y, 2), pl.ds(2 * x, 2))
        return (
            pltpu.make_async_copy(fine_ref.at[sl], fine_v.at[cs], fine_sem.at[step]),
            pltpu.make_async_copy(restr_ref.at[sl], restr_v.at[cs], restr_sem.at[step]),
        )

    owner_copy = pltpu.make_async_copy(owner_hbm, owner_ref, owner_sem)
    owner_copy.start()
    for step in range(CS):
        for c in fine_copies(step):
            c.start()
    links_copy = pltpu.make_async_copy(links_ref.at[0, 0], links_v, links_sem)
    links_copy.start()

    barrier = pltpu.get_barrier_semaphore()
    for d in range(1, NS):
        pl.semaphore_signal(
            barrier, inc=1, device_id={"space": lax.rem(me + d, NS)}, device_id_type=MESH)
    for d in range(1, NT):
        pl.semaphore_signal(
            barrier, inc=1, device_id={"tm": lax.rem(tm + d, NT)}, device_id_type=MESH)

    def find(z, carry):
        acc = jnp.int32(0)
        for s in range(NS):
            acc = jnp.where(owner_ref[s] == z, s, acc)
        source_s[z] = acc
        return carry

    owner_copy.wait()
    lax.fori_loop(0, NS, find, 0)

    for step in range(CS):
        for c in fine_copies(step):
            c.wait()
        cs = site_of(step)
        acc = jnp.zeros((RHS, W), F32)
        for a in range(2):
            for b in range(2):
                for c in range(2):
                    lhs = jnp.concatenate(
                        [fine_v[cs, a, b, c, 0], fine_v[cs, a, b, c, 1]], axis=-1)
                    acc = acc + dot(lhs, restr_v[cs, a, b, c].reshape(2 * W, W))
        own_v[pl.ds(cs * 4, 4)] = acc.reshape(4, 8, W)
    pl.semaphore_wait(barrier, NS - 1 + NT - 1)
    my_slot = my_z * 4 + my_y
    others = pl.ds(0, NS - 1)

    def piece(d):
        target = space_far(d)
        return target, target % NZ * 4 + target // NZ

    for d in range(NS - 1):
        target, slot = piece(d)
        pltpu.make_async_remote_copy(
            src_ref=own_v.at[slot], dst_ref=mid_v.at[me],
            send_sem=up_send, recv_sem=up_recv,
            device_id={"space": target}, device_id_type=MESH).start()
    mid_v[me] = own_v[my_slot]
    drain(mid_v.at[others], up_recv)

    for d in range(NS - 1):
        target = space_far(d)
        pick_v[d] = mid_v[source_s[target]]
        pltpu.make_async_remote_copy(
            src_ref=pick_v.at[d], dst_ref=r_v.at[my_slot],
            send_sem=down_send, recv_sem=down_recv,
            device_id={"space": target}, device_id_type=MESH).start()
    r_v[my_slot] = mid_v[source_s[me]]
    drain(r_v.at[others], down_recv)
    links_copy.wait()

    lane = lax.broadcasted_iota(jnp.int32, (RHS, W), 1)
    row = lax.broadcasted_iota(jnp.int32, (RHS, W), 0)

    def read_r(cs):
        return r_v[pl.ds(4 * cs, 4)].reshape(RHS, W)

    def read_img(it, cs):
        return img_v[it, pl.ds(4 * cs, 4)].reshape(RHS, W)

    def put_img(it, cs, q):
        img_v[it, pl.ds(4 * cs, 4)] = q.reshape(4, 8, W)

    def read_imgh(it, k, cs):
        return imgh_v[it, k, pl.ds(4 * cs, 4)].reshape(RHS, W)

    midq = (midq0_v, midq1_v)

    def back_up(it):
        for d in range(NS - 1):
            target, slot = piece(d)
            pltpu.make_async_remote_copy(
                src_ref=img_v.at[it, slot], dst_ref=midq[it].at[me],
                send_sem=b1_send.at[it], recv_sem=b1_recv.at[it],
                device_id={"space": target}, device_id_type=MESH).start()
        midq[it][me] = img_v[it, my_slot]

    def back_down(it):
        drain(midq[it].at[others], b1_recv.at[it])
        for d in range(NS - 1):
            target = space_far(d)
            pickq_v[it, d] = midq[it][owner_ref[target]]
            pltpu.make_async_remote_copy(
                src_ref=pickq_v.at[it, d], dst_ref=backq_v.at[it, my_slot],
                send_sem=b2_send.at[it], recv_sem=b2_recv.at[it],
                device_id={"space": target}, device_id_type=MESH).start()
        backq_v[it, my_slot] = midq[it][owner_ref[me]]

    halo_to = (
        {"tm": lax.rem(tm + NT - 1, NT)}, {"tm": lax.rem(tm + 1, NT)},
        {"space": lax.rem(me + NS - 1, NS)}, {"space": lax.rem(me + 1, NS)},
    )

    def halo_copy(src, dst, send, recv, k):
        return pltpu.make_async_remote_copy(
            src_ref=src, dst_ref=dst, send_sem=send, recv_sem=recv,
            device_id=halo_to[k], device_id_type=MESH)

    p_halo = [halo_copy(p_v.at[0], ph_v.at[0, k], p_send.at[k], p_recv.at[k], k)
              for k in range(4)]
    low_halo = [halo_copy(low_v, lowh_v.at[k], low_send.at[k], low_recv.at[k], k)
                for k in range(4)]
    img_halo = [[halo_copy(img_v.at[it], imgh_v.at[it, k], img_send.at[it, k],
                           img_recv.at[it, k], k) for k in range(4)] for it in range(2)]

    def pair_copy(it):
        return pltpu.make_async_remote_copy(
            src_ref=part_v.at[it, 0], dst_ref=pair_v.at[it, my_c],
            send_sem=c_send.at[it], recv_sem=c_recv.at[it],
            device_id={"tm": my_x * 2 + 1 - my_c}, device_id_type=MESH)

    ring = (2, 1, 3, 0)
    rows_y = [lax.rem(my_y + dy, NY) * NZ for dy in ring]
    cols_x = [lax.rem(my_x + dx, 4) * 2 + my_c for dx in ring]
    chip = me * 4 + my_x

    def send_chip(it):
        def layer(dz, skip):
            z = lax.rem(my_z + dz, NZ)
            for i in range(16 - skip):
                pltpu.make_async_remote_copy(
                    src_ref=part_v.at[it, 1], dst_ref=sums_v.at[it, chip],
                    send_sem=s_send.at[it], recv_sem=s_recv.at[it],
                    device_id={"space": rows_y[i // 4] + z, "tm": cols_x[i % 4]},
                    device_id_type=MESH).start()

        def one(k, carry):
            layer(far_first(k, NZ), 0)
            return carry

        lax.fori_loop(0, NZ - 1, one, 0)
        layer(0, 1)

    norms, alphas, betas = [], [], []
    for it in range(ITERS):
        if it == 0:
            for cs in range(CS):
                p_v[0, cs] = read_r(cs).astype(BF16)
            for k in range(4):
                p_halo[k].start()
            for cs in range(CS):
                low_v[cs] = (read_r(cs) - p_v[0, cs].astype(F32)).astype(BF16)
            for k in range(4):
                low_halo[k].start()

        def inner(cs):
            y, x = cs // 4, cs % 4
            vy = p_v[it, (1 - y) * 4 + x]
            return [vy, vy, p_v[it, y * 4 + (x + 1) % 4], p_v[it, y * 4 + (x + 3) % 4]]

        def outer(cs):
            return [ph_v[it, k, cs] for k in range(4)]

        if it == 0:
            for cs in range(CS):
                y, x = cs // 4, cs % 4
                put_img(it, cs, dot(p_v[it, cs], links_v[y, x, 0]) + dot(
                    jnp.concatenate(inner(cs), axis=-1),
                    links_v[y, x, pl.ds(5, 4)].reshape(4 * W, W)))
            for k in range(4):
                p_halo[k].wait_recv()
        nprod = it + 2
        prods = [jnp.zeros((RHS, W), F32) for _ in range(nprod)]
        for cs in range(CS):
            y, x = cs // 4, cs % 4
            if it == 0:
                q = read_img(it, cs) + dot(
                    jnp.concatenate(outer(cs), axis=-1),
                    links_v[y, x, pl.ds(1, 4)].reshape(4 * W, W))
            else:
                q = dot(
                    jnp.concatenate([p_v[it, cs]] + outer(cs) + inner(cs), axis=-1),
                    links_v[y, x].reshape(9 * W, W))
            put_img(it, cs, q)
            earlier = [read_img(0, cs), orth_v[cs]] if it == 2 else [read_img(0, cs)] * it
            factors = earlier + [q, read_r(cs)]
            for k in range(nprod):
                prods[k] = prods[k] + q * factors[k]
        packed = jnp.zeros((RHS, W), F32)
        for k in range(nprod):
            total = jnp.sum(prods[k], axis=1, keepdims=True)
            packed = packed + jnp.where(lane == row + RHS * k, total, 0.0)
        mine = jnp.sum(packed, axis=0, keepdims=True)

        part_v[it, 0] = mine
        pair_v[it, my_c] = mine
        pair = pair_copy(it)
        pair.start()
        pair.wait_recv()
        both = pair_v[it, 0] + pair_v[it, 1]
        part_v[it, 1] = both
        sums_v[it, chip] = both
        send_chip(it)
        if it < 2:
            for k in range(4):
                img_halo[it][k].start()
        if it > 0:
            back_down(it - 1)
        if it < 2:
            back_up(it)
        drain(sums_v.at[it, pl.ds(0, CHIPS - 1)], s_recv.at[it])
        totals = jnp.broadcast_to(jnp.sum(sums_v[it], axis=0), (RHS, W))
        cols = [
            jnp.sum(jnp.where(lane == row + RHS * k, totals, 0.0), axis=1, keepdims=True)
            for k in range(nprod)
        ]
        beta = [cols[j] / norms[j] for j in range(it)]
        norm = cols[it]
        for j in range(it):
            norm = norm - beta[j] * cols[j]
        alpha = cols[it + 1] / norm
        norms.append(norm)
        alphas.append(alpha)
        betas.append(beta)
        step = jnp.broadcast_to(alpha, (RHS, W))
        coef = [jnp.broadcast_to(b, (RHS, W)) for b in beta]
        for cs in range(CS):
            q = read_img(it, cs)
            if it > 0:
                q = q - coef[0] * read_img(0, cs)
            if it == 1:
                orth_v[cs] = q
            if it == 2:
                q = q - coef[1] * orth_v[cs]
            new = read_r(cs) - step * q
            if it < ITERS - 1:
                r_v[pl.ds(4 * cs, 4)] = new.reshape(4, 8, W)
                p_v[it + 1, cs] = new.astype(BF16)
            else:
                res_v[cs // 4, cs % 4] = new
        if it < ITERS - 1:
            for k in range(4):
                if it == 0:
                    low_halo[k].wait_recv()
                img_halo[it][k].wait_recv()
                for cs in range(CS):
                    q = read_imgh(it, k, cs)
                    if it == 0:
                        old = ph_v[0, k, cs].astype(F32) + lowh_v[k, cs].astype(F32)
                    else:
                        old = rh_v[k, cs]
                        q = q - coef[0] * read_imgh(0, k, cs)
                    new = old - step * q
                    if it == 0:
                        rh_v[k, cs] = new
                    ph_v[it + 1, k, cs] = new.astype(BF16)

    res_copy = pltpu.make_async_copy(res_v, res_ref.at[0, 0], res_sem)
    res_copy.start()

    c2 = alphas[2]
    c1 = alphas[1] - c2 * betas[2][1]
    c0 = alphas[0] - c1 * betas[1][0] - c2 * betas[2][0]

    wide = lambda c: jnp.broadcast_to(c, (RHS, W))
    w0, w1, w2 = wide(c0), wide(c1), wide(c2)
    s0, s1, b10 = wide(alphas[0]), wide(alphas[1]), wide(betas[1][0])
    for it in range(2):
        drain(backq_v.at[it, others], b2_recv.at[it])
    for cs in range(CS):
        sl = pl.ds(4 * cs, 4)
        r0 = own_v[sl].reshape(RHS, W)
        q0 = backq_v[0, sl].reshape(RHS, W)
        r1 = r0 - s0 * q0
        r2 = r1 - s1 * (backq_v[1, sl].reshape(RHS, W) - b10 * q0)
        dirs = [r.astype(BF16).astype(F32) for r in (r0, r1, r2)]
        fix_v[cs] = (w0 * dirs[0] + w1 * dirs[1] + w2 * dirs[2]).astype(BF16)

    fix_copy = pltpu.make_async_copy(fix_v, fix_ref, fix_sem)
    fix_copy.start()

    drain(own_v.at[others], up_send)
    drain(pick_v.at[others], down_send)
    for k in range(4):
        p_halo[k].wait_send()
        low_halo[k].wait_send()
        for it in range(2):
            img_halo[it][k].wait_send()
    for it in range(ITERS):
        pair_copy(it).wait_send()
        drain(sums_v.at[it, pl.ds(0, CHIPS - 1)], s_send.at[it])
    for it in range(2):
        drain(midq[it].at[others], b1_send.at[it])
        drain(pickq_v.at[it, others], b2_send.at[it])
    res_copy.wait()
    fix_copy.wait()


def prolong_kernel(fix_ref, res_in_ref, restr_ref, corr_ref, res_ref,
                   fix_v, restr_v, out_v, fix_sem, res_sem, restr_sem, out_sem):
    def views(cs):
        y, x = cs // 4, cs % 4
        return (slice(None), slice(None), pl.ds(2 * y, 2), pl.ds(2 * x, 2))

    fix_copy = pltpu.make_async_copy(fix_ref, fix_v, fix_sem)
    fix_copy.start()
    loads = [
        pltpu.make_async_copy(restr_ref.at[views(cs)], restr_v.at[cs], restr_sem.at[cs])
        for cs in range(CS)
    ]
    stores = [
        pltpu.make_async_copy(out_v.at[cs], corr_ref.at[views(cs)], out_sem.at[cs])
        for cs in range(CS)
    ]
    for load in loads:
        load.start()
    res_copy = pltpu.make_async_copy(res_in_ref, res_ref, res_sem)
    res_copy.start()
    fix_copy.wait()
    for cs in range(CS):
        loads[cs].wait()
        fix = fix_v[cs]
        for a in range(2):
            for b in range(2):
                for c in range(2):
                    both = lax.dot_general(
                        fix, restr_v[cs, a, b, c].reshape(2 * W, W),
                        (((1,), (1,)), ((), ())), preferred_element_type=F32)
                    out_v[cs, a, b, c, 0] = both[:, :W]
                    out_v[cs, a, b, c, 1] = both[:, W:]
        stores[cs].start()
    res_copy.wait()
    for store in stores:
        store.wait()


def body(fine_residual, restriction, coarse_links, plane_owner):
    dma = pltpu.SemaphoreType.DMA
    hbm = pl.BlockSpec(memory_space=pl.ANY)
    res_shape = jax.ShapeDtypeStruct((1, 1, 2, 4, RHS, W), F32)
    plane = (NS, 8, W)
    fix, res = pl.pallas_call(
        cycle_kernel,
        out_shape=(jax.ShapeDtypeStruct((CS, RHS, W), BF16), res_shape),
        in_specs=[hbm, hbm, hbm, hbm],
        out_specs=(hbm, hbm),
        scratch_shapes=[
            pltpu.VMEM((CS, 2, 2, 2, 2, RHS, W), BF16),
            pltpu.VMEM((CS, 2, 2, 2, 2, W, W), BF16),
            pltpu.VMEM((2, 4, 9, W, W), BF16),
            pltpu.VMEM((CS, RHS, W), BF16),
            pltpu.VMEM((2, 4, RHS, W), F32),
            pltpu.VMEM(plane, F32),
            pltpu.VMEM(plane, F32),
            pltpu.VMEM(plane, F32),
            pltpu.VMEM(plane, F32),
            pltpu.VMEM((CS, RHS, W), BF16),
            pltpu.VMEM((ITERS, CS, RHS, W), BF16),
            pltpu.VMEM((ITERS,) + plane, F32),
            pltpu.VMEM((CS, RHS, W), F32),
            pltpu.VMEM((ITERS, 4, CS, RHS, W), BF16),
            pltpu.VMEM((4, CS, RHS, W), BF16),
            pltpu.VMEM((2, 4) + plane, F32),
            pltpu.VMEM((4, CS, RHS, W), F32),
            pltpu.VMEM(plane, F32),
            pltpu.VMEM(plane, F32),
            pltpu.VMEM((2,) + plane, F32),
            pltpu.VMEM((2,) + plane, F32),
            pltpu.VMEM((ITERS, 2, 1, W), F32),
            pltpu.VMEM((ITERS, 2, 1, W), F32),
            pltpu.VMEM((ITERS, CHIPS, 1, W), F32),
            pltpu.SMEM((NS,), jnp.int32),
            pltpu.SMEM((NS,), jnp.int32),
            dma(()), dma(()), dma(()), dma((CS,)), dma((CS,)), dma(()),
            dma(()), dma(()), dma(()), dma(()),
            dma((4,)), dma((4,)), dma((4,)), dma((4,)), dma((2, 4)), dma((2, 4)),
            dma((ITERS,)), dma((ITERS,)), dma((ITERS,)), dma((ITERS,)),
            dma((2,)), dma((2,)), dma((2,)), dma((2,)),
        ],
        compiler_params=pltpu.CompilerParams(
            collective_id=0, has_side_effects=True, vmem_limit_bytes=60 * MIB),
        name="coarse_cycle",
    )(plane_owner, fine_residual, restriction, coarse_links)
    return pl.pallas_call(
        prolong_kernel,
        out_shape=(jax.ShapeDtypeStruct(fine_residual.shape, F32), res_shape),
        in_specs=[hbm, hbm, hbm],
        out_specs=(hbm, hbm),
        scratch_shapes=[
            pltpu.VMEM((CS, RHS, W), BF16),
            pltpu.VMEM((CS, 2, 2, 2, 2, W, W), BF16),
            pltpu.VMEM((CS, 2, 2, 2, 2, RHS, W), F32),
            dma(()), dma(()), dma((CS,)), dma((CS,)),
        ],
        compiler_params=pltpu.CompilerParams(vmem_limit_bytes=60 * MIB),
        name="prolong",
    )(fix, res, restriction)


def solution(mesh):
    placed = (
        P("tm", "space", None, None, None, None),
        P("tm", "space", None, None, None, None),
        P("tm", "space", None, None, None, None, None),
        P(),
    )
    return jax.shard_map(
        body,
        mesh=mesh,
        in_specs=placed,
        out_specs=(
            P("tm", "space", None, None, None, None),
            P("tm", "space", None, None, None, None),
        ),
        check_vma=False,
    )
```

```python
import jax
import jax.numpy as jnp
from jax import lax
from jax.experimental import pallas as pl
from jax.experimental.pallas import tpu as pltpu
from jax.sharding import PartitionSpec as P

ITERS = 3
NS = 32
NT = 8
NY, NZ = 4, 8
CHIPS = NS * NT // 2
CS = 8
RHS = 32
W = 128
F32 = jnp.float32
BF16 = jnp.bfloat16
MESH = pl.DeviceIdType.MESH
MIB = 1024 * 1024


def dot(a, b):
    return jnp.dot(a, b, preferred_element_type=F32)


def drain(ref, sem):
    pltpu.make_async_copy(ref, ref, sem).wait()


def far_first(i, n):
    return n // 2 + (1 - 2 * (i % 2)) * ((i + 1) // 2)


def cycle_kernel(
    owner_hbm, fine_ref, restr_ref, links_ref, fix_ref, res_ref,
    fine_v, restr_v, links_v, fix_v, res_v,
    own_v, mid_v, pick_v, r_v, low_v, p_v, img_v, orth_v,
    ph_v, lowh_v, imgh_v, rh_v,
    qb_v, midb_v, pickb_v, back_v, part_v, pair_v, sums_v, owner_ref, source_s,
    owner_sem, fix_sem, res_sem, fine_sem, restr_sem, links_sem,
    up_send, up_recv, down_send, down_recv,
    p_send, p_recv, low_send, low_recv, img_send, img_recv,
    c_send, c_recv, s_send, s_recv, b1_send, b1_recv, b2_send, b2_recv,
):
    me = lax.axis_index("space")
    tm = lax.axis_index("tm")
    my_y, my_z = me // NZ, me % NZ
    my_x, my_c = tm // 2, tm % 2

    by_z = [lax.rem(my_z + far_first(k, NZ), NZ) for k in range(NZ)]
    by_y = [lax.rem(my_y + far_first(k, NY), NY) for k in range(NY)]

    def space_far(d):
        return by_y[d % NY] * NZ + by_z[d // NY]

    def site_of(step):
        return lax.rem(my_z + far_first(step, NZ), CS)

    def fine_copies(step):
        cs = site_of(step)
        y, x = cs // 4, cs % 4
        sl = (slice(None), slice(None), pl.ds(2 * y, 2), pl.ds(2 * x, 2))
        return (
            pltpu.make_async_copy(fine_ref.at[sl], fine_v.at[cs], fine_sem.at[step]),
            pltpu.make_async_copy(restr_ref.at[sl], restr_v.at[cs], restr_sem.at[step]),
        )

    owner_copy = pltpu.make_async_copy(owner_hbm, owner_ref, owner_sem)
    owner_copy.start()
    for step in range(CS):
        for c in fine_copies(step):
            c.start()
    links_copy = pltpu.make_async_copy(links_ref.at[0, 0], links_v, links_sem)
    links_copy.start()

    barrier = pltpu.get_barrier_semaphore()
    for d in range(1, NS):
        pl.semaphore_signal(
            barrier, inc=1, device_id={"space": lax.rem(me + d, NS)}, device_id_type=MESH)
    for d in range(1, NT):
        pl.semaphore_signal(
            barrier, inc=1, device_id={"tm": lax.rem(tm + d, NT)}, device_id_type=MESH)

    def find(z, carry):
        acc = jnp.int32(0)
        for s in range(NS):
            acc = jnp.where(owner_ref[s] == z, s, acc)
        source_s[z] = acc
        return carry

    owner_copy.wait()
    lax.fori_loop(0, NS, find, 0)

    for step in range(CS):
        for c in fine_copies(step):
            c.wait()
        cs = site_of(step)
        acc = jnp.zeros((RHS, W), F32)
        for a in range(2):
            for b in range(2):
                for c in range(2):
                    lhs = jnp.concatenate(
                        [fine_v[cs, a, b, c, 0], fine_v[cs, a, b, c, 1]], axis=-1)
                    acc = acc + dot(lhs, restr_v[cs, a, b, c].reshape(2 * W, W))
        own_v[pl.ds(cs * 4, 4)] = acc.reshape(4, 8, W)
    pl.semaphore_wait(barrier, NS - 1 + NT - 1)
    my_slot = my_z * 4 + my_y
    others = pl.ds(0, NS - 1)

    for d in range(NS - 1):
        target, slot = space_far(d), by_z[d // NY] * 4 + by_y[d % NY]
        pltpu.make_async_remote_copy(
            src_ref=own_v.at[slot], dst_ref=mid_v.at[me],
            send_sem=up_send, recv_sem=up_recv,
            device_id={"space": target}, device_id_type=MESH).start()
    mid_v[me] = own_v[my_slot]
    drain(mid_v.at[others], up_recv)

    for d in range(NS - 1):
        target = space_far(d)
        pick_v[d] = mid_v[source_s[target]]
        pltpu.make_async_remote_copy(
            src_ref=pick_v.at[d], dst_ref=r_v.at[my_slot],
            send_sem=down_send, recv_sem=down_recv,
            device_id={"space": target}, device_id_type=MESH).start()
    r_v[my_slot] = mid_v[source_s[me]]
    drain(r_v.at[others], down_recv)
    links_copy.wait()

    lane = lax.broadcasted_iota(jnp.int32, (RHS, W), 1)
    row = lax.broadcasted_iota(jnp.int32, (RHS, W), 0)

    def read_r(cs):
        return r_v[pl.ds(4 * cs, 4)].reshape(RHS, W)

    def read_img(it, cs):
        return img_v[it, pl.ds(4 * cs, 4)].reshape(RHS, W)

    def put_img(it, cs, q):
        img_v[it, pl.ds(4 * cs, 4)] = q.reshape(4, 8, W)

    def read_imgh(it, k, cs):
        return imgh_v[it, k, pl.ds(4 * cs, 4)].reshape(RHS, W)

    parity = lax.rem(me, 2)
    half_z = [lax.rem(my_z // 2 + k, NZ // 2) for k in (2, 1, 3, 0)]

    def back_up(it):
        for cs in range(CS):
            qb_v[it, pl.ds(2 * cs, 2)] = read_img(it, cs).astype(BF16).reshape(2, 16, W)
        for d in range(16):
            y, zh = by_y[d // 4], half_z[d % 4]
            h = y * 4 + zh

            def send(y=y, zh=zh, h=h):
                pltpu.make_async_remote_copy(
                    src_ref=qb_v.at[it, h], dst_ref=midb_v.at[me],
                    send_sem=b1_send.at[it], recv_sem=b1_recv,
                    device_id={"space": y * NZ + 2 * zh + it}, device_id_type=MESH).start()

            if d < 15:
                send()
            else:
                pl.when(parity != it)(send)

                @pl.when(parity == it)
                def _():
                    midb_v[me] = qb_v[it, h]

    def back_down():
        drain(midb_v.at[others], b1_recv)
        for d in range(NS - 1):
            pickb_v[d] = midb_v[owner_ref[space_far(d)]]
        for d in range(NS - 1):
            pltpu.make_async_remote_copy(
                src_ref=pickb_v.at[d], dst_ref=back_v.at[parity, me // 2],
                send_sem=b2_send, recv_sem=b2_recv.at[parity],
                device_id={"space": space_far(d)}, device_id_type=MESH).start()
        back_v[parity, me // 2] = midb_v[owner_ref[me]]

    def drain_back(sems):
        for it in range(2):
            @pl.when(parity == it)
            def _():
                drain(back_v.at[it, pl.ds(0, 15)], sems.at[it])

            @pl.when(parity != it)
            def _():
                drain(back_v.at[it], sems.at[it])

    halo_to = (
        {"tm": lax.rem(tm + NT - 1, NT)}, {"tm": lax.rem(tm + 1, NT)},
        {"space": lax.rem(me + NS - 1, NS)}, {"space": lax.rem(me + 1, NS)},
    )

    def halo_copy(src, dst, send, recv, k):
        return pltpu.make_async_remote_copy(
            src_ref=src, dst_ref=dst, send_sem=send, recv_sem=recv,
            device_id=halo_to[k], device_id_type=MESH)

    p_halo = [halo_copy(p_v.at[0], ph_v.at[0, k], p_send.at[k], p_recv.at[k], k)
              for k in range(4)]
    low_halo = [halo_copy(low_v, lowh_v.at[k], low_send.at[k], low_recv.at[k], k)
                for k in range(4)]
    img_halo = [[halo_copy(img_v.at[it], imgh_v.at[it, k], img_send.at[it, k],
                           img_recv.at[it, k], k) for k in range(4)] for it in range(2)]

    def pair_copy(it):
        return pltpu.make_async_remote_copy(
            src_ref=part_v.at[it, 0], dst_ref=pair_v.at[it, my_c],
            send_sem=c_send.at[it], recv_sem=c_recv.at[it],
            device_id={"tm": my_x * 2 + 1 - my_c}, device_id_type=MESH)

    ring = (2, 1, 3, 0)
    rows_y = [lax.rem(my_y + dy, NY) * NZ for dy in ring]
    cols_x = [lax.rem(my_x + dx, 4) * 2 + my_c for dx in ring]
    chip = me * 4 + my_x

    def send_chip(it):
        def layer(dz, skip):
            z = lax.rem(my_z + dz, NZ)
            for i in range(16 - skip):
                pltpu.make_async_remote_copy(
                    src_ref=part_v.at[it, 1], dst_ref=sums_v.at[it, chip],
                    send_sem=s_send.at[it], recv_sem=s_recv.at[it],
                    device_id={"space": rows_y[i // 4] + z, "tm": cols_x[i % 4]},
                    device_id_type=MESH).start()

        def one(k, carry):
            layer(far_first(k, NZ), 0)
            return carry

        lax.fori_loop(0, NZ - 1, one, 0)
        layer(0, 1)

    norms, alphas, betas = [], [], []
    for it in range(ITERS):
        if it == 0:
            for cs in range(CS):
                p_v[0, cs] = read_r(cs).astype(BF16)
            for k in range(4):
                p_halo[k].start()
            for cs in range(CS):
                low_v[cs] = (read_r(cs) - p_v[0, cs].astype(F32)).astype(BF16)
            for k in range(4):
                low_halo[k].start()

        def inner(cs):
            y, x = cs // 4, cs % 4
            vy = p_v[it, (1 - y) * 4 + x]
            return [vy, vy, p_v[it, y * 4 + (x + 1) % 4], p_v[it, y * 4 + (x + 3) % 4]]

        def outer(cs):
            return [ph_v[it, k, cs] for k in range(4)]

        if it == 0:
            for cs in range(CS):
                y, x = cs // 4, cs % 4
                put_img(it, cs, dot(p_v[it, cs], links_v[y, x, 0]) + dot(
                    jnp.concatenate(inner(cs), axis=-1),
                    links_v[y, x, pl.ds(5, 4)].reshape(4 * W, W)))
            for k in range(4):
                p_halo[k].wait_recv()
        nprod = it + 2
        prods = [jnp.zeros((RHS, W), F32) for _ in range(nprod)]
        for cs in range(CS):
            y, x = cs // 4, cs % 4
            if it == 0:
                q = read_img(it, cs) + dot(
                    jnp.concatenate(outer(cs), axis=-1),
                    links_v[y, x, pl.ds(1, 4)].reshape(4 * W, W))
            else:
                q = dot(
                    jnp.concatenate([p_v[it, cs]] + outer(cs) + inner(cs), axis=-1),
                    links_v[y, x].reshape(9 * W, W))
            put_img(it, cs, q)
            earlier = [read_img(0, cs), orth_v[cs]] if it == 2 else [read_img(0, cs)] * it
            factors = earlier + [q, read_r(cs)]
            for k in range(nprod):
                prods[k] = prods[k] + q * factors[k]
        packed = jnp.zeros((RHS, W), F32)
        for k in range(nprod):
            total = jnp.sum(prods[k], axis=1, keepdims=True)
            packed = packed + jnp.where(lane == row + RHS * k, total, 0.0)
        mine = jnp.sum(packed, axis=0, keepdims=True)

        part_v[it, 0] = mine
        pair_v[it, my_c] = mine
        pair = pair_copy(it)
        pair.start()
        if it == 1:
            back_up(0)
        pair.wait_recv()
        both = pair_v[it, 0] + pair_v[it, 1]
        part_v[it, 1] = both
        sums_v[it, chip] = both
        send_chip(it)
        if it < 2:
            for k in range(4):
                img_halo[it][k].start()
        if it == 1:
            back_up(1)
        if it == 2:
            back_down()
        drain(sums_v.at[it, pl.ds(0, CHIPS - 1)], s_recv.at[it])
        totals = jnp.broadcast_to(jnp.sum(sums_v[it], axis=0), (RHS, W))
        cols = [
            jnp.sum(jnp.where(lane == row + RHS * k, totals, 0.0), axis=1, keepdims=True)
            for k in range(nprod)
        ]
        beta = [cols[j] / norms[j] for j in range(it)]
        norm = cols[it]
        for j in range(it):
            norm = norm - beta[j] * cols[j]
        alpha = cols[it + 1] / norm
        norms.append(norm)
        alphas.append(alpha)
        betas.append(beta)
        step = jnp.broadcast_to(alpha, (RHS, W))
        coef = [jnp.broadcast_to(b, (RHS, W)) for b in beta]
        for cs in range(CS):
            q = read_img(it, cs)
            if it > 0:
                q = q - coef[0] * read_img(0, cs)
            if it == 1:
                orth_v[cs] = q
            if it == 2:
                q = q - coef[1] * orth_v[cs]
            new = read_r(cs) - step * q
            if it < ITERS - 1:
                r_v[pl.ds(4 * cs, 4)] = new.reshape(4, 8, W)
                p_v[it + 1, cs] = new.astype(BF16)
            else:
                res_v[cs // 4, cs % 4] = new
        if it < ITERS - 1:
            for k in range(4):
                if it == 0:
                    low_halo[k].wait_recv()
                img_halo[it][k].wait_recv()
                for cs in range(CS):
                    q = read_imgh(it, k, cs)
                    if it == 0:
                        old = ph_v[0, k, cs].astype(F32) + lowh_v[k, cs].astype(F32)
                    else:
                        old = rh_v[k, cs]
                        q = q - coef[0] * read_imgh(0, k, cs)
                    new = old - step * q
                    if it == 0:
                        rh_v[k, cs] = new
                    ph_v[it + 1, k, cs] = new.astype(BF16)

    res_copy = pltpu.make_async_copy(res_v, res_ref.at[0, 0], res_sem)
    res_copy.start()

    c2 = alphas[2]
    c1 = alphas[1] - c2 * betas[2][1]
    c0 = alphas[0] - c1 * betas[1][0] - c2 * betas[2][0]

    wide = lambda c: jnp.broadcast_to(c, (RHS, W))
    w0, w1, w2 = wide(c0), wide(c1), wide(c2)
    s0, s1, b10 = wide(alphas[0]), wide(alphas[1]), wide(betas[1][0])
    drain_back(b2_recv)
    for cs in range(CS):
        sl = pl.ds(4 * cs, 4)
        r0 = own_v[sl].reshape(RHS, W)
        q0 = back_v[0, pl.ds(2 * cs, 2)].reshape(RHS, W).astype(F32)
        q1 = back_v[1, pl.ds(2 * cs, 2)].reshape(RHS, W).astype(F32)
        r1 = r0 - s0 * q0
        r2 = r1 - s1 * (q1 - b10 * q0)
        dirs = [r.astype(BF16).astype(F32) for r in (r0, r1, r2)]
        fix_v[cs] = (w0 * dirs[0] + w1 * dirs[1] + w2 * dirs[2]).astype(BF16)

    fix_copy = pltpu.make_async_copy(fix_v, fix_ref, fix_sem)
    fix_copy.start()

    drain(own_v.at[others], up_send)
    drain(pick_v.at[others], down_send)
    for k in range(4):
        p_halo[k].wait_send()
        low_halo[k].wait_send()
        for it in range(2):
            img_halo[it][k].wait_send()
    for it in range(ITERS):
        pair_copy(it).wait_send()
        drain(sums_v.at[it, pl.ds(0, CHIPS - 1)], s_send.at[it])
    drain_back(b1_send)
    drain(pickb_v.at[others], b2_send)
    res_copy.wait()
    fix_copy.wait()


def prolong_kernel(fix_ref, res_in_ref, restr_ref, corr_ref, res_ref,
                   fix_v, res_v, restr_v, out_v, fix_sem, res_sem, restr_sem, out_sem):
    def views(cs):
        y, x = cs // 4, cs % 4
        return (slice(None), slice(None), pl.ds(2 * y, 2), pl.ds(2 * x, 2))

    fix_copy = pltpu.make_async_copy(fix_ref, fix_v, fix_sem)
    fix_copy.start()
    loads = [
        pltpu.make_async_copy(restr_ref.at[views(cs)], restr_v.at[cs], restr_sem.at[cs])
        for cs in range(CS)
    ]
    stores = [
        pltpu.make_async_copy(out_v.at[cs], corr_ref.at[views(cs)], out_sem.at[cs])
        for cs in range(CS)
    ]
    for load in loads:
        load.start()
    res_in = pltpu.make_async_copy(res_in_ref, res_v, res_sem.at[0])
    res_in.start()
    res_out = pltpu.make_async_copy(res_v, res_ref, res_sem.at[1])
    fix_copy.wait()
    for cs in range(CS):
        loads[cs].wait()
        fix = fix_v[cs]
        for a in range(2):
            for b in range(2):
                for c in range(2):
                    both = lax.dot_general(
                        fix, restr_v[cs, a, b, c].reshape(2 * W, W),
                        (((1,), (1,)), ((), ())), preferred_element_type=F32)
                    out_v[cs, a, b, c, 0] = both[:, :W]
                    out_v[cs, a, b, c, 1] = both[:, W:]
        stores[cs].start()
        if cs == 0:
            res_in.wait()
            res_out.start()
    res_out.wait()
    for store in stores:
        store.wait()


def body(fine_residual, restriction, coarse_links, plane_owner):
    dma = pltpu.SemaphoreType.DMA
    hbm = pl.BlockSpec(memory_space=pl.ANY)
    res_shape = jax.ShapeDtypeStruct((1, 1, 2, 4, RHS, W), F32)
    plane = (NS, 8, W)
    fix, res = pl.pallas_call(
        cycle_kernel,
        out_shape=(jax.ShapeDtypeStruct((CS, RHS, W), BF16), res_shape),
        in_specs=[hbm, hbm, hbm, hbm],
        out_specs=(hbm, hbm),
        scratch_shapes=[
            pltpu.VMEM((CS, 2, 2, 2, 2, RHS, W), BF16),
            pltpu.VMEM((CS, 2, 2, 2, 2, W, W), BF16),
            pltpu.VMEM((2, 4, 9, W, W), BF16),
            pltpu.VMEM((CS, RHS, W), BF16),
            pltpu.VMEM((2, 4, RHS, W), F32),
            pltpu.VMEM(plane, F32),
            pltpu.VMEM(plane, F32),
            pltpu.VMEM(plane, F32),
            pltpu.VMEM(plane, F32),
            pltpu.VMEM((CS, RHS, W), BF16),
            pltpu.VMEM((ITERS, CS, RHS, W), BF16),
            pltpu.VMEM((ITERS,) + plane, F32),
            pltpu.VMEM((CS, RHS, W), F32),
            pltpu.VMEM((ITERS, 4, CS, RHS, W), BF16),
            pltpu.VMEM((4, CS, RHS, W), BF16),
            pltpu.VMEM((2, 4) + plane, F32),
            pltpu.VMEM((4, CS, RHS, W), F32),
            pltpu.VMEM((2, 16, 16, W), BF16),
            pltpu.VMEM((NS, 16, W), BF16),
            pltpu.VMEM((NS, 16, W), BF16),
            pltpu.VMEM((2, 16, 16, W), BF16),
            pltpu.VMEM((ITERS, 2, 1, W), F32),
            pltpu.VMEM((ITERS, 2, 1, W), F32),
            pltpu.VMEM((ITERS, CHIPS, 1, W), F32),
            pltpu.SMEM((NS,), jnp.int32),
            pltpu.SMEM((NS,), jnp.int32),
            dma(()), dma(()), dma(()), dma((CS,)), dma((CS,)), dma(()),
            dma(()), dma(()), dma(()), dma(()),
            dma((4,)), dma((4,)), dma((4,)), dma((4,)), dma((2, 4)), dma((2, 4)),
            dma((ITERS,)), dma((ITERS,)), dma((ITERS,)), dma((ITERS,)),
            dma((2,)), dma(()), dma(()), dma((2,)),
        ],
        compiler_params=pltpu.CompilerParams(
            collective_id=0, has_side_effects=True, vmem_limit_bytes=60 * MIB),
        name="coarse_cycle",
    )(plane_owner, fine_residual, restriction, coarse_links)
    return pl.pallas_call(
        prolong_kernel,
        out_shape=(jax.ShapeDtypeStruct(fine_residual.shape, F32), res_shape),
        in_specs=[hbm, hbm, hbm],
        out_specs=(hbm, hbm),
        scratch_shapes=[
            pltpu.VMEM((CS, RHS, W), BF16),
            pltpu.VMEM((1, 1, 2, 4, RHS, W), F32),
            pltpu.VMEM((CS, 2, 2, 2, 2, W, W), BF16),
            pltpu.VMEM((CS, 2, 2, 2, 2, RHS, W), F32),
            dma(()), dma((2,)), dma((CS,)), dma((CS,)),
        ],
        compiler_params=pltpu.CompilerParams(vmem_limit_bytes=60 * MIB),
        name="prolong",
    )(fix, res, restriction)


def solution(mesh):
    placed = (
        P("tm", "space", None, None, None, None),
        P("tm", "space", None, None, None, None),
        P("tm", "space", None, None, None, None, None),
        P(),
    )
    return jax.shard_map(
        body,
        mesh=mesh,
        in_specs=placed,
        out_specs=(
            P("tm", "space", None, None, None, None),
            P("tm", "space", None, None, None, None),
        ),
        check_vma=False,
    )
```

```python
import jax
import jax.numpy as jnp
from jax import lax
from jax.experimental import pallas as pl
from jax.experimental.pallas import tpu as pltpu
from jax.sharding import PartitionSpec as P

ITERS = 3
NS = 32
NT = 8
NY, NZ = 4, 8
CHIPS = NS * NT // 2
CS = 8
RHS = 32
W = 128
F32 = jnp.float32
BF16 = jnp.bfloat16
MESH = pl.DeviceIdType.MESH
MIB = 1024 * 1024


def dot(a, b):
    return jnp.dot(a, b, preferred_element_type=F32)


def drain(ref, sem):
    pltpu.make_async_copy(ref, ref, sem).wait()


def far_first(i, n):
    return n // 2 + (1 - 2 * (i % 2)) * ((i + 1) // 2)


def cycle_kernel(
    owner_hbm, fine_ref, restr_ref, links_ref, fix_ref, res_ref,
    fine_v, restr_v, links_v, fix_v, res_v,
    own_v, mid_v, pick_v, r_v, low_v, p_v, img_v, orth_v,
    ph_v, lowh_v, imgh_v, rh_v,
    qb_v, midb_v, pickb_v, back_v, part_v, pair_v, sums_v, owner_ref, source_s,
    owner_sem, fix_sem, res_sem, fine_sem, restr_sem, links_sem,
    up_send, up_recv, down_send, down_recv,
    p_send, p_recv, low_send, low_recv, img_send, img_recv,
    c_send, c_recv, s_send, s_recv, b1_send, b1_recv, b2_send, b2_recv,
):
    me = lax.axis_index("space")
    tm = lax.axis_index("tm")
    my_y, my_z = me // NZ, me % NZ
    my_x, my_c = tm // 2, tm % 2

    by_z = [lax.rem(my_z + far_first(k, NZ), NZ) for k in range(NZ)]
    by_y = [lax.rem(my_y + far_first(k, NY), NY) for k in range(NY)]

    def space_far(d):
        return by_y[d % NY] * NZ + by_z[d // NY]

    barrier = pltpu.get_barrier_semaphore()
    for d in range(NS - 1):
        pl.semaphore_signal(
            barrier, inc=1, device_id={"space": space_far(d)}, device_id_type=MESH)
    for d in (4, 5, 2, 3, 6, 7, 1):
        pl.semaphore_signal(
            barrier, inc=1, device_id={"tm": lax.rem(tm + d, NT)}, device_id_type=MESH)

    def site_of(step):
        return by_z[step]

    def fine_copies(step):
        cs = site_of(step)
        y, x = cs // 4, cs % 4
        sl = (slice(None), slice(None), pl.ds(2 * y, 2), pl.ds(2 * x, 2))
        return (
            pltpu.make_async_copy(fine_ref.at[sl], fine_v.at[cs], fine_sem.at[step]),
            pltpu.make_async_copy(restr_ref.at[sl], restr_v.at[cs], restr_sem.at[step]),
        )

    owner_copy = pltpu.make_async_copy(owner_hbm, owner_ref, owner_sem)
    owner_copy.start()
    for step in range(CS):
        for c in fine_copies(step):
            c.start()
    links_copy = pltpu.make_async_copy(links_ref.at[0, 0], links_v, links_sem)
    links_copy.start()

    def find(z, carry):
        acc = jnp.int32(0)
        for s in range(NS):
            acc = jnp.where(owner_ref[s] == z, s, acc)
        source_s[z] = acc
        return carry

    owner_copy.wait()
    lax.fori_loop(0, NS, find, 0)

    for step in range(CS):
        for c in fine_copies(step):
            c.wait()
        cs = site_of(step)
        acc = jnp.zeros((RHS, W), F32)
        for a in range(2):
            for b in range(2):
                for c in range(2):
                    lhs = jnp.concatenate(
                        [fine_v[cs, a, b, c, 0], fine_v[cs, a, b, c, 1]], axis=-1)
                    acc = acc + dot(lhs, restr_v[cs, a, b, c].reshape(2 * W, W))
        own_v[pl.ds(cs * 4, 4)] = acc.reshape(4, 8, W)
    pl.semaphore_wait(barrier, NS - 1 + NT - 1)
    my_slot = my_z * 4 + my_y
    others = pl.ds(0, NS - 1)

    for d in range(NS - 1):
        target, slot = space_far(d), by_z[d // NY] * 4 + by_y[d % NY]
        pltpu.make_async_remote_copy(
            src_ref=own_v.at[slot], dst_ref=mid_v.at[me],
            send_sem=up_send, recv_sem=up_recv,
            device_id={"space": target}, device_id_type=MESH).start()
    mid_v[me] = own_v[my_slot]
    drain(mid_v.at[others], up_recv)

    for d in range(NS - 1):
        pick_v[d] = mid_v[source_s[space_far(d)]]
    for d in range(NS - 1):
        target = space_far(d)
        pltpu.make_async_remote_copy(
            src_ref=pick_v.at[d], dst_ref=r_v.at[my_slot],
            send_sem=down_send, recv_sem=down_recv,
            device_id={"space": target}, device_id_type=MESH).start()
    r_v[my_slot] = mid_v[source_s[me]]
    drain(r_v.at[others], down_recv)
    links_copy.wait()

    lane = lax.broadcasted_iota(jnp.int32, (RHS, W), 1)
    row = lax.broadcasted_iota(jnp.int32, (RHS, W), 0)

    def read_r(cs):
        return r_v[pl.ds(4 * cs, 4)].reshape(RHS, W)

    def read_img(it, cs):
        return img_v[it, pl.ds(4 * cs, 4)].reshape(RHS, W)

    def put_img(it, cs, q):
        img_v[it, pl.ds(4 * cs, 4)] = q.reshape(4, 8, W)

    def read_imgh(it, k, cs):
        return imgh_v[it, k, pl.ds(4 * cs, 4)].reshape(RHS, W)

    parity = lax.rem(me, 2)
    half_z = [lax.rem(my_z // 2 + k, NZ // 2) for k in (2, 1, 3, 0)]

    def back_up(it):
        for cs in range(CS):
            qb_v[it, pl.ds(2 * cs, 2)] = read_img(it, cs).astype(BF16).reshape(2, 16, W)
        for d in range(16):
            y, zh = by_y[d // 4], half_z[d % 4]
            h = y * 4 + zh

            def send(y=y, zh=zh, h=h):
                pltpu.make_async_remote_copy(
                    src_ref=qb_v.at[it, h], dst_ref=midb_v.at[me],
                    send_sem=b1_send.at[it], recv_sem=b1_recv,
                    device_id={"space": y * NZ + 2 * zh + it}, device_id_type=MESH).start()

            if d < 15:
                send()
            else:
                pl.when(parity != it)(send)

                @pl.when(parity == it)
                def _():
                    midb_v[me] = qb_v[it, h]

    def back_down():
        drain(midb_v.at[others], b1_recv)
        for d in range(NS - 1):
            pickb_v[d] = midb_v[owner_ref[space_far(d)]]
        for d in range(NS - 1):
            pltpu.make_async_remote_copy(
                src_ref=pickb_v.at[d], dst_ref=back_v.at[parity, me // 2],
                send_sem=b2_send, recv_sem=b2_recv.at[parity],
                device_id={"space": space_far(d)}, device_id_type=MESH).start()
        back_v[parity, me // 2] = midb_v[owner_ref[me]]

    def drain_back(sems):
        for it in range(2):
            @pl.when(parity == it)
            def _():
                drain(back_v.at[it, pl.ds(0, 15)], sems.at[it])

            @pl.when(parity != it)
            def _():
                drain(back_v.at[it], sems.at[it])

    halo_to = (
        {"tm": lax.rem(tm + NT - 1, NT)}, {"tm": lax.rem(tm + 1, NT)},
        {"space": lax.rem(me + NS - 1, NS)}, {"space": lax.rem(me + 1, NS)},
    )

    def halo_copy(src, dst, send, recv, k):
        return pltpu.make_async_remote_copy(
            src_ref=src, dst_ref=dst, send_sem=send, recv_sem=recv,
            device_id=halo_to[k], device_id_type=MESH)

    p_halo = [halo_copy(p_v.at[0], ph_v.at[0, k], p_send.at[k], p_recv.at[k], k)
              for k in range(4)]
    low_halo = [halo_copy(low_v, lowh_v.at[k], low_send.at[k], low_recv.at[k], k)
                for k in range(4)]
    img_halo = [[halo_copy(img_v.at[it], imgh_v.at[it, k], img_send.at[it, k],
                           img_recv.at[it, k], k) for k in range(4)] for it in range(2)]

    def pair_copy(it):
        return pltpu.make_async_remote_copy(
            src_ref=part_v.at[it, 0], dst_ref=pair_v.at[it, my_c],
            send_sem=c_send.at[it], recv_sem=c_recv.at[it],
            device_id={"tm": my_x * 2 + 1 - my_c}, device_id_type=MESH)

    ring = (2, 1, 3, 0)
    rows_y = [lax.rem(my_y + dy, NY) * NZ for dy in ring]
    cols_x = [lax.rem(my_x + dx, 4) * 2 + my_c for dx in ring]
    chip = me * 4 + my_x

    def send_chip(it):
        def layer(dz, skip):
            z = lax.rem(my_z + dz, NZ)
            for i in range(16 - skip):
                pltpu.make_async_remote_copy(
                    src_ref=part_v.at[it, 1], dst_ref=sums_v.at[it, chip],
                    send_sem=s_send.at[it], recv_sem=s_recv.at[it],
                    device_id={"space": rows_y[i // 4] + z, "tm": cols_x[i % 4]},
                    device_id_type=MESH).start()

        def one(k, carry):
            layer(far_first(k, NZ), 0)
            return carry

        lax.fori_loop(0, NZ - 1, one, 0)
        layer(0, 1)

    norms, alphas, betas = [], [], []
    for it in range(ITERS):
        if it == 0:
            for cs in range(CS):
                p_v[0, cs] = read_r(cs).astype(BF16)
            for k in range(4):
                p_halo[k].start()
            for cs in range(CS):
                low_v[cs] = (read_r(cs) - p_v[0, cs].astype(F32)).astype(BF16)
            for k in range(4):
                low_halo[k].start()

        def inner(cs):
            y, x = cs // 4, cs % 4
            vy = p_v[it, (1 - y) * 4 + x]
            return [vy, vy, p_v[it, y * 4 + (x + 1) % 4], p_v[it, y * 4 + (x + 3) % 4]]

        def outer(cs):
            return [ph_v[it, k, cs] for k in range(4)]

        if it == 0:
            for cs in range(CS):
                y, x = cs // 4, cs % 4
                put_img(it, cs, dot(p_v[it, cs], links_v[y, x, 0]) + dot(
                    jnp.concatenate(inner(cs), axis=-1),
                    links_v[y, x, pl.ds(5, 4)].reshape(4 * W, W)))
            for k in range(4):
                p_halo[k].wait_recv()
        nprod = it + 2
        prods = [jnp.zeros((RHS, W), F32) for _ in range(nprod)]
        for cs in range(CS):
            y, x = cs // 4, cs % 4
            if it == 0:
                q = read_img(it, cs) + dot(
                    jnp.concatenate(outer(cs), axis=-1),
                    links_v[y, x, pl.ds(1, 4)].reshape(4 * W, W))
            else:
                q = dot(
                    jnp.concatenate([p_v[it, cs]] + outer(cs) + inner(cs), axis=-1),
                    links_v[y, x].reshape(9 * W, W))
            put_img(it, cs, q)
            earlier = [read_img(0, cs), orth_v[cs]] if it == 2 else [read_img(0, cs)] * it
            factors = earlier + [q, read_r(cs)]
            for k in range(nprod):
                prods[k] = prods[k] + q * factors[k]
        packed = jnp.zeros((RHS, W), F32)
        for k in range(nprod):
            total = jnp.sum(prods[k], axis=1, keepdims=True)
            packed = packed + jnp.where(lane == row + RHS * k, total, 0.0)
        mine = jnp.sum(packed, axis=0, keepdims=True)

        part_v[it, 0] = mine
        pair_v[it, my_c] = mine
        pair = pair_copy(it)
        pair.start()
        if it == 1:
            back_up(0)
        pair.wait_recv()
        both = pair_v[it, 0] + pair_v[it, 1]
        part_v[it, 1] = both
        sums_v[it, chip] = both
        send_chip(it)
        if it < 2:
            for k in range(4):
                img_halo[it][k].start()
        if it == 1:
            back_up(1)
        if it == 2:
            back_down()
        drain(sums_v.at[it, pl.ds(0, CHIPS - 1)], s_recv.at[it])
        totals = jnp.broadcast_to(jnp.sum(sums_v[it], axis=0), (RHS, W))
        cols = [
            jnp.sum(jnp.where(lane == row + RHS * k, totals, 0.0), axis=1, keepdims=True)
            for k in range(nprod)
        ]
        beta = [cols[j] / norms[j] for j in range(it)]
        norm = cols[it]
        for j in range(it):
            norm = norm - beta[j] * cols[j]
        alpha = cols[it + 1] / norm
        norms.append(norm)
        alphas.append(alpha)
        betas.append(beta)
        step = jnp.broadcast_to(alpha, (RHS, W))
        coef = [jnp.broadcast_to(b, (RHS, W)) for b in beta]
        for cs in range(CS):
            q = read_img(it, cs)
            if it > 0:
                q = q - coef[0] * read_img(0, cs)
            if it == 1:
                orth_v[cs] = q
            if it == 2:
                q = q - coef[1] * orth_v[cs]
            new = read_r(cs) - step * q
            if it < ITERS - 1:
                r_v[pl.ds(4 * cs, 4)] = new.reshape(4, 8, W)
                p_v[it + 1, cs] = new.astype(BF16)
            else:
                res_v[cs // 4, cs % 4] = new
        if it < ITERS - 1:
            for k in range(4):
                if it == 0:
                    low_halo[k].wait_recv()
                img_halo[it][k].wait_recv()
                for cs in range(CS):
                    q = read_imgh(it, k, cs)
                    if it == 0:
                        old = ph_v[0, k, cs].astype(F32) + lowh_v[k, cs].astype(F32)
                    else:
                        old = rh_v[k, cs]
                        q = q - coef[0] * read_imgh(0, k, cs)
                    new = old - step * q
                    if it == 0:
                        rh_v[k, cs] = new
                    ph_v[it + 1, k, cs] = new.astype(BF16)

    res_copy = pltpu.make_async_copy(res_v, res_ref.at[0, 0], res_sem)
    res_copy.start()

    c2 = alphas[2]
    c1 = alphas[1] - c2 * betas[2][1]
    c0 = alphas[0] - c1 * betas[1][0] - c2 * betas[2][0]

    wide = lambda c: jnp.broadcast_to(c, (RHS, W))
    w0, w1, w2 = wide(c0), wide(c1), wide(c2)
    s0, s1, b10 = wide(alphas[0]), wide(alphas[1]), wide(betas[1][0])
    drain_back(b2_recv)
    for cs in range(CS):
        sl = pl.ds(4 * cs, 4)
        r0 = own_v[sl].reshape(RHS, W)
        q0 = back_v[0, pl.ds(2 * cs, 2)].reshape(RHS, W).astype(F32)
        q1 = back_v[1, pl.ds(2 * cs, 2)].reshape(RHS, W).astype(F32)
        r1 = r0 - s0 * q0
        r2 = r1 - s1 * (q1 - b10 * q0)
        dirs = [r.astype(BF16).astype(F32) for r in (r0, r1, r2)]
        fix_v[cs] = (w0 * dirs[0] + w1 * dirs[1] + w2 * dirs[2]).astype(BF16)

    fix_copy = pltpu.make_async_copy(fix_v, fix_ref, fix_sem)
    fix_copy.start()

    drain(own_v.at[others], up_send)
    drain(pick_v.at[others], down_send)
    for k in range(4):
        p_halo[k].wait_send()
        low_halo[k].wait_send()
        for it in range(2):
            img_halo[it][k].wait_send()
    for it in range(ITERS):
        pair_copy(it).wait_send()
        drain(sums_v.at[it, pl.ds(0, CHIPS - 1)], s_send.at[it])
    drain_back(b1_send)
    drain(pickb_v.at[others], b2_send)
    res_copy.wait()
    fix_copy.wait()


def prolong_kernel(fix_ref, res_in_ref, restr_ref, corr_ref, res_ref,
                   fix_v, res_v, restr_v, out_v, fix_sem, res_sem, restr_sem, out_sem):
    def views(cs):
        y, x = cs // 4, cs % 4
        return (slice(None), slice(None), pl.ds(2 * y, 2), pl.ds(2 * x, 2))

    fix_copy = pltpu.make_async_copy(fix_ref, fix_v, fix_sem)
    fix_copy.start()
    loads = [
        pltpu.make_async_copy(restr_ref.at[views(cs)], restr_v.at[cs], restr_sem.at[cs])
        for cs in range(CS)
    ]
    stores = [
        pltpu.make_async_copy(out_v.at[cs], corr_ref.at[views(cs)], out_sem.at[cs])
        for cs in range(CS)
    ]
    for load in loads:
        load.start()
    res_in = pltpu.make_async_copy(res_in_ref, res_v, res_sem.at[0])
    res_in.start()
    res_out = pltpu.make_async_copy(res_v, res_ref, res_sem.at[1])
    fix_copy.wait()
    for group in ((0,), (1, 2), (3, 4), (5, 6), (7,)):
        for cs in group:
            loads[cs].wait()
        for cs in group:
            fix = fix_v[cs]
            for a in range(2):
                for b in range(2):
                    for c in range(2):
                        both = lax.dot_general(
                            fix, restr_v[cs, a, b, c].reshape(2 * W, W),
                            (((1,), (1,)), ((), ())), preferred_element_type=F32)
                        out_v[cs, a, b, c, 0] = both[:, :W]
                        out_v[cs, a, b, c, 1] = both[:, W:]
        for cs in group:
            stores[cs].start()
    res_in.wait()
    res_out.start()
    for store in stores:
        store.wait()
    res_out.wait()


def body(fine_residual, restriction, coarse_links, plane_owner):
    dma = pltpu.SemaphoreType.DMA
    hbm = pl.BlockSpec(memory_space=pl.ANY)
    res_shape = jax.ShapeDtypeStruct((1, 1, 2, 4, RHS, W), F32)
    plane = (NS, 8, W)
    fix, res = pl.pallas_call(
        cycle_kernel,
        out_shape=(jax.ShapeDtypeStruct((CS, RHS, W), BF16), res_shape),
        in_specs=[hbm, hbm, hbm, hbm],
        out_specs=(hbm, hbm),
        scratch_shapes=[
            pltpu.VMEM((CS, 2, 2, 2, 2, RHS, W), BF16),
            pltpu.VMEM((CS, 2, 2, 2, 2, W, W), BF16),
            pltpu.VMEM((2, 4, 9, W, W), BF16),
            pltpu.VMEM((CS, RHS, W), BF16),
            pltpu.VMEM((2, 4, RHS, W), F32),
            pltpu.VMEM(plane, F32),
            pltpu.VMEM(plane, F32),
            pltpu.VMEM(plane, F32),
            pltpu.VMEM(plane, F32),
            pltpu.VMEM((CS, RHS, W), BF16),
            pltpu.VMEM((ITERS, CS, RHS, W), BF16),
            pltpu.VMEM((ITERS,) + plane, F32),
            pltpu.VMEM((CS, RHS, W), F32),
            pltpu.VMEM((ITERS, 4, CS, RHS, W), BF16),
            pltpu.VMEM((4, CS, RHS, W), BF16),
            pltpu.VMEM((2, 4) + plane, F32),
            pltpu.VMEM((4, CS, RHS, W), F32),
            pltpu.VMEM((2, 16, 16, W), BF16),
            pltpu.VMEM((NS, 16, W), BF16),
            pltpu.VMEM((NS, 16, W), BF16),
            pltpu.VMEM((2, 16, 16, W), BF16),
            pltpu.VMEM((ITERS, 2, 1, W), F32),
            pltpu.VMEM((ITERS, 2, 1, W), F32),
            pltpu.VMEM((ITERS, CHIPS, 1, W), F32),
            pltpu.SMEM((NS,), jnp.int32),
            pltpu.SMEM((NS,), jnp.int32),
            dma(()), dma(()), dma(()), dma((CS,)), dma((CS,)), dma(()),
            dma(()), dma(()), dma(()), dma(()),
            dma((4,)), dma((4,)), dma((4,)), dma((4,)), dma((2, 4)), dma((2, 4)),
            dma((ITERS,)), dma((ITERS,)), dma((ITERS,)), dma((ITERS,)),
            dma((2,)), dma(()), dma(()), dma((2,)),
        ],
        compiler_params=pltpu.CompilerParams(
            collective_id=0, has_side_effects=True, vmem_limit_bytes=60 * MIB),
        name="coarse_cycle",
    )(plane_owner, fine_residual, restriction, coarse_links)
    return pl.pallas_call(
        prolong_kernel,
        out_shape=(jax.ShapeDtypeStruct(fine_residual.shape, F32), res_shape),
        in_specs=[hbm, hbm, hbm],
        out_specs=(hbm, hbm),
        scratch_shapes=[
            pltpu.VMEM((CS, RHS, W), BF16),
            pltpu.VMEM((1, 1, 2, 4, RHS, W), F32),
            pltpu.VMEM((CS, 2, 2, 2, 2, W, W), BF16),
            pltpu.VMEM((CS, 2, 2, 2, 2, RHS, W), F32),
            dma(()), dma((2,)), dma((CS,)), dma((CS,)),
        ],
        compiler_params=pltpu.CompilerParams(vmem_limit_bytes=60 * MIB),
        name="prolong",
    )(fix, res, restriction)


def solution(mesh):
    placed = (
        P("tm", "space", None, None, None, None),
        P("tm", "space", None, None, None, None),
        P("tm", "space", None, None, None, None, None),
        P(),
    )
    return jax.shard_map(
        body,
        mesh=mesh,
        in_specs=placed,
        out_specs=(
            P("tm", "space", None, None, None, None),
            P("tm", "space", None, None, None, None),
        ),
        check_vma=False,
    )
```

```python
import jax
import jax.numpy as jnp
from jax import lax
from jax.experimental import pallas as pl
from jax.experimental.pallas import tpu as pltpu
from jax.sharding import PartitionSpec as P

ITERS = 3
NS = 32
NT = 8
NY, NZ = 4, 8
CHIPS = NS * NT // 2
CS = 8
RHS = 32
W = 128
F32 = jnp.float32
BF16 = jnp.bfloat16
MESH = pl.DeviceIdType.MESH
MIB = 1024 * 1024


def dot(a, b):
    return jnp.dot(a, b, preferred_element_type=F32)


def drain(ref, sem):
    pltpu.make_async_copy(ref, ref, sem).wait()


def far_first(i, n):
    return n // 2 + (1 - 2 * (i % 2)) * ((i + 1) // 2)


def cycle_kernel(
    owner_hbm, fine_ref, restr_ref, links_ref, fix_ref, res_ref,
    fine_v, restr_v, links_v, fix_v, res_v,
    own_v, mid_v, pick_v, r_v, low_v, p_v, img_v, orth_v,
    ph_v, lowh_v, imgh_v, rh_v,
    qb_v, midb_v, pickb_v, back_v, part_v, pair_v, sums_v, owner_ref, source_s,
    owner_sem, fix_sem, res_sem, fine_sem, restr_sem, links_sem,
    up_send, up_recv, down_send, down_recv,
    p_send, p_recv, low_send, low_recv, img_send, img_recv,
    c_send, c_recv, s_send, s_recv, b1_send, b1_recv, b2_send, b2_recv,
):
    me = lax.axis_index("space")
    tm = lax.axis_index("tm")
    my_y, my_z = me // NZ, me % NZ
    my_x, my_c = tm // 2, tm % 2

    by_z = [lax.rem(my_z + far_first(k, NZ), NZ) for k in range(NZ)]
    by_y = [lax.rem(my_y + far_first(k, NY), NY) for k in range(NY)]

    def space_far(d):
        return by_y[d % NY] * NZ + by_z[d // NY]

    barrier = pltpu.get_barrier_semaphore()
    for d in range(NS - 1):
        pl.semaphore_signal(
            barrier, inc=1, device_id={"space": space_far(d)}, device_id_type=MESH)
    for d in (4, 5, 2, 3, 6, 7, 1):
        pl.semaphore_signal(
            barrier, inc=1, device_id={"tm": lax.rem(tm + d, NT)}, device_id_type=MESH)

    def site_of(step):
        return by_z[step]

    def fine_copies(step):
        cs = site_of(step)
        y, x = cs // 4, cs % 4
        sl = (slice(None), slice(None), pl.ds(2 * y, 2), pl.ds(2 * x, 2))
        return (
            pltpu.make_async_copy(fine_ref.at[sl], fine_v.at[cs], fine_sem.at[step]),
            pltpu.make_async_copy(restr_ref.at[sl], restr_v.at[cs], restr_sem.at[step]),
        )

    owner_copy = pltpu.make_async_copy(owner_hbm, owner_ref, owner_sem)
    owner_copy.start()
    for step in range(CS):
        for c in fine_copies(step):
            c.start()
    links_copy = pltpu.make_async_copy(links_ref.at[0, 0], links_v, links_sem)
    links_copy.start()

    def find(z, carry):
        acc = jnp.int32(0)
        for s in range(NS):
            acc = jnp.where(owner_ref[s] == z, s, acc)
        source_s[z] = acc
        return carry

    owner_copy.wait()
    lax.fori_loop(0, NS, find, 0)

    for step in range(CS):
        for c in fine_copies(step):
            c.wait()
        cs = site_of(step)
        acc = jnp.zeros((RHS, W), F32)
        for a in range(2):
            for b in range(2):
                for c in range(2):
                    lhs = jnp.concatenate(
                        [fine_v[cs, a, b, c, 0], fine_v[cs, a, b, c, 1]], axis=-1)
                    acc = acc + dot(lhs, restr_v[cs, a, b, c].reshape(2 * W, W))
        own_v[pl.ds(cs * 4, 4)] = acc.reshape(4, 8, W)
    pl.semaphore_wait(barrier, NS - 1 + NT - 1)
    my_slot = my_z * 4 + my_y
    others = pl.ds(0, NS - 1)

    for d in range(NS - 1):
        target, slot = space_far(d), by_z[d // NY] * 4 + by_y[d % NY]
        pltpu.make_async_remote_copy(
            src_ref=own_v.at[slot], dst_ref=mid_v.at[me],
            send_sem=up_send, recv_sem=up_recv,
            device_id={"space": target}, device_id_type=MESH).start()
    mid_v[me] = own_v[my_slot]
    drain(mid_v.at[others], up_recv)

    for d in range(NS - 1):
        pick_v[d] = mid_v[source_s[space_far(d)]]
    for d in range(NS - 1):
        target = space_far(d)
        pltpu.make_async_remote_copy(
            src_ref=pick_v.at[d], dst_ref=r_v.at[my_slot],
            send_sem=down_send, recv_sem=down_recv,
            device_id={"space": target}, device_id_type=MESH).start()
    r_v[my_slot] = mid_v[source_s[me]]
    drain(r_v.at[others], down_recv)
    links_copy.wait()

    lane = lax.broadcasted_iota(jnp.int32, (RHS, W), 1)
    row = lax.broadcasted_iota(jnp.int32, (RHS, W), 0)

    def read_r(cs):
        return r_v[pl.ds(4 * cs, 4)].reshape(RHS, W)

    def read_img(it, cs):
        return img_v[it, pl.ds(4 * cs, 4)].reshape(RHS, W)

    def put_img(it, cs, q):
        img_v[it, pl.ds(4 * cs, 4)] = q.reshape(4, 8, W)

    def read_imgh(it, k, cs):
        return imgh_v[it, k, pl.ds(4 * cs, 4)].reshape(RHS, W)

    parity = lax.rem(me, 2)
    half_z = [lax.rem(my_z // 2 + k, NZ // 2) for k in (2, 1, 3, 0)]

    def back_up(it):
        for cs in range(CS):
            qb_v[it, pl.ds(2 * cs, 2)] = read_img(it, cs).astype(BF16).reshape(2, 16, W)
        for d in range(16):
            y, zh = by_y[d // 4], half_z[d % 4]
            h = y * 4 + zh

            def send(y=y, zh=zh, h=h):
                pltpu.make_async_remote_copy(
                    src_ref=qb_v.at[it, h], dst_ref=midb_v.at[me],
                    send_sem=b1_send.at[it], recv_sem=b1_recv,
                    device_id={"space": y * NZ + 2 * zh + it}, device_id_type=MESH).start()

            if d < 15:
                send()
            else:
                pl.when(parity != it)(send)

                @pl.when(parity == it)
                def _():
                    midb_v[me] = qb_v[it, h]

    def back_down():
        drain(midb_v.at[others], b1_recv)
        for d in range(NS - 1):
            pickb_v[d] = midb_v[owner_ref[space_far(d)]]
        for d in range(NS - 1):
            pltpu.make_async_remote_copy(
                src_ref=pickb_v.at[d], dst_ref=back_v.at[parity, me // 2],
                send_sem=b2_send, recv_sem=b2_recv.at[parity],
                device_id={"space": space_far(d)}, device_id_type=MESH).start()
        back_v[parity, me // 2] = midb_v[owner_ref[me]]

    def drain_back(sems):
        for it in range(2):
            @pl.when(parity == it)
            def _():
                drain(back_v.at[it, pl.ds(0, 15)], sems.at[it])

            @pl.when(parity != it)
            def _():
                drain(back_v.at[it], sems.at[it])

    halo_to = (
        {"tm": lax.rem(tm + NT - 1, NT)}, {"tm": lax.rem(tm + 1, NT)},
        {"space": lax.rem(me + NS - 1, NS)}, {"space": lax.rem(me + 1, NS)},
    )

    def halo_copy(src, dst, send, recv, k):
        return pltpu.make_async_remote_copy(
            src_ref=src, dst_ref=dst, send_sem=send, recv_sem=recv,
            device_id=halo_to[k], device_id_type=MESH)

    p_halo = [halo_copy(p_v.at[0], ph_v.at[0, k], p_send.at[k], p_recv.at[k], k)
              for k in range(4)]
    low_halo = [halo_copy(low_v, lowh_v.at[k], low_send.at[k], low_recv.at[k], k)
                for k in range(4)]
    img_halo = [[halo_copy(img_v.at[it], imgh_v.at[it, k], img_send.at[it, k],
                           img_recv.at[it, k], k) for k in range(4)] for it in range(2)]

    def pair_copy(it):
        return pltpu.make_async_remote_copy(
            src_ref=part_v.at[it, 0], dst_ref=pair_v.at[it, my_c],
            send_sem=c_send.at[it], recv_sem=c_recv.at[it],
            device_id={"tm": my_x * 2 + 1 - my_c}, device_id_type=MESH)

    ring = (2, 1, 3, 0)
    rows_y = [lax.rem(my_y + dy, NY) * NZ for dy in ring]
    cols_x = [lax.rem(my_x + dx, 4) * 2 + my_c for dx in ring]
    chip = me * 4 + my_x

    def send_chip(it):
        def layer(dz, skip):
            z = lax.rem(my_z + dz, NZ)
            for i in range(16 - skip):
                pltpu.make_async_remote_copy(
                    src_ref=part_v.at[it, 1], dst_ref=sums_v.at[it, chip],
                    send_sem=s_send.at[it], recv_sem=s_recv.at[it],
                    device_id={"space": rows_y[i // 4] + z, "tm": cols_x[i % 4]},
                    device_id_type=MESH).start()

        def one(k, carry):
            layer(far_first(k, NZ), 0)
            return carry

        lax.fori_loop(0, NZ - 1, one, 0)
        layer(0, 1)

    norms, alphas, betas = [], [], []
    for it in range(ITERS):
        if it == 0:
            for cs in range(CS):
                p_v[0, cs] = read_r(cs).astype(BF16)
            for k in range(4):
                p_halo[k].start()
            for cs in range(CS):
                low_v[cs] = (read_r(cs) - p_v[0, cs].astype(F32)).astype(BF16)
            for k in range(4):
                low_halo[k].start()

        def inner(cs):
            y, x = cs // 4, cs % 4
            vy = p_v[it, (1 - y) * 4 + x]
            return [vy, vy, p_v[it, y * 4 + (x + 1) % 4], p_v[it, y * 4 + (x + 3) % 4]]

        def outer(cs):
            return [ph_v[it, k, cs] for k in range(4)]

        for cs in range(CS):
            y, x = cs // 4, cs % 4
            put_img(it, cs, dot(p_v[it, cs], links_v[y, x, 0]) + dot(
                jnp.concatenate(inner(cs), axis=-1),
                links_v[y, x, pl.ds(5, 4)].reshape(4 * W, W)))
        if it == 0:
            for k in range(4):
                p_halo[k].wait_recv()
        else:
            last = it - 1
            coef = [jnp.broadcast_to(b, (RHS, W)) for b in betas[last]]
            step = jnp.broadcast_to(alphas[last], (RHS, W))
            for k in range(4):
                if last == 0:
                    low_halo[k].wait_recv()
                img_halo[last][k].wait_recv()
                for cs in range(CS):
                    q = read_imgh(last, k, cs)
                    if last == 0:
                        old = ph_v[0, k, cs].astype(F32) + lowh_v[k, cs].astype(F32)
                    else:
                        old = rh_v[k, cs]
                        q = q - coef[0] * read_imgh(0, k, cs)
                    new = old - step * q
                    if last == 0:
                        rh_v[k, cs] = new
                    ph_v[it, k, cs] = new.astype(BF16)
        nprod = it + 2
        prods = [jnp.zeros((RHS, W), F32) for _ in range(nprod)]
        for cs in range(CS):
            y, x = cs // 4, cs % 4
            q = read_img(it, cs) + dot(
                jnp.concatenate(outer(cs), axis=-1),
                links_v[y, x, pl.ds(1, 4)].reshape(4 * W, W))
            put_img(it, cs, q)
            earlier = [read_img(0, cs), orth_v[cs]] if it == 2 else [read_img(0, cs)] * it
            factors = earlier + [q, read_r(cs)]
            for k in range(nprod):
                prods[k] = prods[k] + q * factors[k]
        packed = jnp.zeros((RHS, W), F32)
        for k in range(nprod):
            total = jnp.sum(prods[k], axis=1, keepdims=True)
            packed = packed + jnp.where(lane == row + RHS * k, total, 0.0)
        mine = jnp.sum(packed, axis=0, keepdims=True)

        part_v[it, 0] = mine
        pair_v[it, my_c] = mine
        pair = pair_copy(it)
        pair.start()
        if it == 1:
            back_up(0)
        pair.wait_recv()
        both = pair_v[it, 0] + pair_v[it, 1]
        part_v[it, 1] = both
        sums_v[it, chip] = both
        send_chip(it)
        if it < 2:
            for k in (2, 3, 0, 1):
                img_halo[it][k].start()
        if it == 1:
            back_up(1)
        if it == 2:
            back_down()
        drain(sums_v.at[it, pl.ds(0, CHIPS - 1)], s_recv.at[it])
        totals = jnp.broadcast_to(jnp.sum(sums_v[it], axis=0), (RHS, W))
        cols = [
            jnp.sum(jnp.where(lane == row + RHS * k, totals, 0.0), axis=1, keepdims=True)
            for k in range(nprod)
        ]
        beta = [cols[j] / norms[j] for j in range(it)]
        norm = cols[it]
        for j in range(it):
            norm = norm - beta[j] * cols[j]
        alpha = cols[it + 1] / norm
        norms.append(norm)
        alphas.append(alpha)
        betas.append(beta)
        step = jnp.broadcast_to(alpha, (RHS, W))
        coef = [jnp.broadcast_to(b, (RHS, W)) for b in beta]
        for cs in range(CS):
            q = read_img(it, cs)
            if it > 0:
                q = q - coef[0] * read_img(0, cs)
            if it == 1:
                orth_v[cs] = q
            if it == 2:
                q = q - coef[1] * orth_v[cs]
            new = read_r(cs) - step * q
            if it < ITERS - 1:
                r_v[pl.ds(4 * cs, 4)] = new.reshape(4, 8, W)
                p_v[it + 1, cs] = new.astype(BF16)
            else:
                res_v[cs // 4, cs % 4] = new

    res_copy = pltpu.make_async_copy(res_v, res_ref.at[0, 0], res_sem)
    res_copy.start()

    c2 = alphas[2]
    c1 = alphas[1] - c2 * betas[2][1]
    c0 = alphas[0] - c1 * betas[1][0] - c2 * betas[2][0]

    wide = lambda c: jnp.broadcast_to(c, (RHS, W))
    w0, w1, w2 = wide(c0), wide(c1), wide(c2)
    s0, s1, b10 = wide(alphas[0]), wide(alphas[1]), wide(betas[1][0])
    drain_back(b2_recv)
    for cs in range(CS):
        sl = pl.ds(4 * cs, 4)
        r0 = own_v[sl].reshape(RHS, W)
        q0 = back_v[0, pl.ds(2 * cs, 2)].reshape(RHS, W).astype(F32)
        q1 = back_v[1, pl.ds(2 * cs, 2)].reshape(RHS, W).astype(F32)
        r1 = r0 - s0 * q0
        r2 = r1 - s1 * (q1 - b10 * q0)
        dirs = [r.astype(BF16).astype(F32) for r in (r0, r1, r2)]
        fix_v[cs] = (w0 * dirs[0] + w1 * dirs[1] + w2 * dirs[2]).astype(BF16)

    fix_copy = pltpu.make_async_copy(fix_v, fix_ref, fix_sem)
    fix_copy.start()

    drain(own_v.at[others], up_send)
    drain(pick_v.at[others], down_send)
    for k in range(4):
        p_halo[k].wait_send()
        low_halo[k].wait_send()
        for it in range(2):
            img_halo[it][k].wait_send()
    for it in range(ITERS):
        pair_copy(it).wait_send()
        drain(sums_v.at[it, pl.ds(0, CHIPS - 1)], s_send.at[it])
    drain_back(b1_send)
    drain(pickb_v.at[others], b2_send)
    res_copy.wait()
    fix_copy.wait()


def prolong_kernel(fix_ref, res_in_ref, restr_ref, corr_ref, res_ref,
                   fix_v, res_v, restr_v, out_v, fix_sem, res_sem, restr_sem, out_sem):
    def views(cs):
        y, x = cs // 4, cs % 4
        return (slice(None), slice(None), pl.ds(2 * y, 2), pl.ds(2 * x, 2))

    fix_copy = pltpu.make_async_copy(fix_ref, fix_v, fix_sem)
    fix_copy.start()
    loads = [
        pltpu.make_async_copy(restr_ref.at[views(cs)], restr_v.at[cs], restr_sem.at[cs])
        for cs in range(CS)
    ]
    stores = [
        pltpu.make_async_copy(out_v.at[cs], corr_ref.at[views(cs)], out_sem.at[cs])
        for cs in range(CS)
    ]
    for load in loads:
        load.start()
    res_in = pltpu.make_async_copy(res_in_ref, res_v, res_sem.at[0])
    res_in.start()
    res_out = pltpu.make_async_copy(res_v, res_ref, res_sem.at[1])
    fix_copy.wait()
    for group in ((0,), (1, 2), (3, 4), (5, 6), (7,)):
        for cs in group:
            loads[cs].wait()
        for cs in group:
            fix = fix_v[cs]
            for a in range(2):
                for b in range(2):
                    for c in range(2):
                        both = lax.dot_general(
                            fix, restr_v[cs, a, b, c].reshape(2 * W, W),
                            (((1,), (1,)), ((), ())), preferred_element_type=F32)
                        out_v[cs, a, b, c, 0] = both[:, :W]
                        out_v[cs, a, b, c, 1] = both[:, W:]
        for cs in group:
            stores[cs].start()
    res_in.wait()
    res_out.start()
    for store in stores:
        store.wait()
    res_out.wait()


def body(fine_residual, restriction, coarse_links, plane_owner):
    dma = pltpu.SemaphoreType.DMA
    hbm = pl.BlockSpec(memory_space=pl.ANY)
    res_shape = jax.ShapeDtypeStruct((1, 1, 2, 4, RHS, W), F32)
    plane = (NS, 8, W)
    fix, res = pl.pallas_call(
        cycle_kernel,
        out_shape=(jax.ShapeDtypeStruct((CS, RHS, W), BF16), res_shape),
        in_specs=[hbm, hbm, hbm, hbm],
        out_specs=(hbm, hbm),
        scratch_shapes=[
            pltpu.VMEM((CS, 2, 2, 2, 2, RHS, W), BF16),
            pltpu.VMEM((CS, 2, 2, 2, 2, W, W), BF16),
            pltpu.VMEM((2, 4, 9, W, W), BF16),
            pltpu.VMEM((CS, RHS, W), BF16),
            pltpu.VMEM((2, 4, RHS, W), F32),
            pltpu.VMEM(plane, F32),
            pltpu.VMEM(plane, F32),
            pltpu.VMEM(plane, F32),
            pltpu.VMEM(plane, F32),
            pltpu.VMEM((CS, RHS, W), BF16),
            pltpu.VMEM((ITERS, CS, RHS, W), BF16),
            pltpu.VMEM((ITERS,) + plane, F32),
            pltpu.VMEM((CS, RHS, W), F32),
            pltpu.VMEM((ITERS, 4, CS, RHS, W), BF16),
            pltpu.VMEM((4, CS, RHS, W), BF16),
            pltpu.VMEM((2, 4) + plane, F32),
            pltpu.VMEM((4, CS, RHS, W), F32),
            pltpu.VMEM((2, 16, 16, W), BF16),
            pltpu.VMEM((NS, 16, W), BF16),
            pltpu.VMEM((NS, 16, W), BF16),
            pltpu.VMEM((2, 16, 16, W), BF16),
            pltpu.VMEM((ITERS, 2, 1, W), F32),
            pltpu.VMEM((ITERS, 2, 1, W), F32),
            pltpu.VMEM((ITERS, CHIPS, 1, W), F32),
            pltpu.SMEM((NS,), jnp.int32),
            pltpu.SMEM((NS,), jnp.int32),
            dma(()), dma(()), dma(()), dma((CS,)), dma((CS,)), dma(()),
            dma(()), dma(()), dma(()), dma(()),
            dma((4,)), dma((4,)), dma((4,)), dma((4,)), dma((2, 4)), dma((2, 4)),
            dma((ITERS,)), dma((ITERS,)), dma((ITERS,)), dma((ITERS,)),
            dma((2,)), dma(()), dma(()), dma((2,)),
        ],
        compiler_params=pltpu.CompilerParams(
            collective_id=0, has_side_effects=True, vmem_limit_bytes=60 * MIB),
        name="coarse_cycle",
    )(plane_owner, fine_residual, restriction, coarse_links)
    return pl.pallas_call(
        prolong_kernel,
        out_shape=(jax.ShapeDtypeStruct(fine_residual.shape, F32), res_shape),
        in_specs=[hbm, hbm, hbm],
        out_specs=(hbm, hbm),
        scratch_shapes=[
            pltpu.VMEM((CS, RHS, W), BF16),
            pltpu.VMEM((1, 1, 2, 4, RHS, W), F32),
            pltpu.VMEM((CS, 2, 2, 2, 2, W, W), BF16),
            pltpu.VMEM((CS, 2, 2, 2, 2, RHS, W), F32),
            dma(()), dma((2,)), dma((CS,)), dma((CS,)),
        ],
        compiler_params=pltpu.CompilerParams(vmem_limit_bytes=60 * MIB),
        name="prolong",
    )(fix, res, restriction)


def solution(mesh):
    placed = (
        P("tm", "space", None, None, None, None),
        P("tm", "space", None, None, None, None),
        P("tm", "space", None, None, None, None, None),
        P(),
    )
    return jax.shard_map(
        body,
        mesh=mesh,
        in_specs=placed,
        out_specs=(
            P("tm", "space", None, None, None, None),
            P("tm", "space", None, None, None, None),
        ),
        check_vma=False,
    )
```
